128 devices in a mesh: cuts: 2 (over z_hi), dp: 64 (over x, y, z_lo, core).
Axes of the slice: x: 4, y: 4, z: 4 (z_hi: 2, z_lo: 2; z = z_hi * 2 + z_lo), core: 2. Of those that a mesh axis runs over, the one named last changes fastest.
Arguments:
- llm_grad: bfloat16 [294912, 1792], P(('cuts', 'dp')), may hold values from -6 to 6
- route_slot: int32 [294912], P(('cuts', 'dp')), may hold values from -1 to 1535, as said below
- route_row: int32 [294912], P(('cuts', 'dp')), may hold values from -1 to 767, as said below
- pre_act: bfloat16 [98304, 2560], P(('cuts', 'dp')), may hold values from -6 to 6
- down_weight: bfloat16 [2560, 1792], replicated, may hold values from -0.125 to 0.125
Outputs:
- d_pre: bfloat16 [98304, 2560], P(('cuts', 'dp'))
- w_grad: float32 [2560, 1792], P('dp')
The draws below stay inside these ranges and needn't reach their ends.
Inputs may be any that keep to these rules, and one draw needn't show every extreme that they name: `route_slot`: within one half's 64 x 2304 rows, a value s >= 0 sends the row to owner s // 24 of that half as its slot s % 24; on one device the values are distinct, and those to one owner are 0 to c - 1 for some c <= 24; -1 marks a text row. In every draw some device sends exactly 24 rows to some owner. `route_row`: -1 exactly where route_slot is -1; otherwise the row among the owner's image tokens; within a half each row of each owner is named exactly once.
All inputs are finite; a program needn't handle non-finite values.
Results may differ from the reference program's by a relative error of at most 0.0029.
Values may be sent and summed in bfloat16 or wider, within the bound.
No kernel may reach another device: no remote copies, remote signals or barrier semaphores. Data moves between devices by JAX's collectives and lax.ppermute only.
A program may use at most 128 MiB of HBM per device.

```python
import jax
import jax.numpy as jnp
from jax import lax

F = 1792
H = 2560
IMG = 768
LLM_ROWS = 2304
N_CUTS = 2
N_DP = 64


def route_slice(slice_key):
    owners = N_DP
    mean_load = IMG // N_DP
    slot_cap = 2 * mean_load
    keys = jax.random.split(slice_key, 5)
    ranking = jax.random.permutation(keys[0], owners).astype(jnp.int32)
    rank_of = jnp.zeros((owners,), jnp.int32).at[ranking].set(jnp.arange(owners, dtype=jnp.int32))
    base = jnp.where(rank_of < owners // 4, 2 * mean_load, jnp.where(rank_of < 3 * owners // 4, 3 * mean_load // 4, mean_load // 2)).astype(jnp.int32)
    heavy_pick = ranking[jax.random.randint(keys[1], (owners,), 0, owners // 4)]
    light_pick = ranking[3 * owners // 4 + jax.random.randint(keys[2], (owners,), 0, owners // 4)]
    senders = jnp.arange(owners, dtype=jnp.int32)
    load = jnp.broadcast_to(base[None, :], (owners, owners))
    load = jnp.where(senders[None, :] == heavy_pick[:, None], mean_load // 2, jnp.where(senders[None, :] == light_pick[:, None], 2 * mean_load, load)).astype(jnp.int32)
    owner_start = jnp.cumsum(load, axis=1) - load
    sender_start = jnp.cumsum(load, axis=0) - load
    row_perm = jax.vmap(lambda k: jax.random.permutation(k, IMG))(jax.random.split(keys[3], owners)).astype(jnp.int32)
    sender_perm = jax.vmap(lambda k: jax.random.permutation(k, LLM_ROWS))(jax.random.split(keys[4], owners)).astype(jnp.int32)
    owner_grid = jnp.arange(owners, dtype=jnp.int32)[:, None, None]
    sender_grid = jnp.arange(owners, dtype=jnp.int32)[None, :, None]
    slot_grid = jnp.arange(slot_cap, dtype=jnp.int32)[None, None, :]
    valid = slot_grid < load[:, :, None]
    owner_place = jnp.minimum(owner_start[:, :, None] + slot_grid, IMG - 1)
    owner_row = row_perm[jnp.broadcast_to(owner_grid, owner_place.shape), owner_place]
    sender_place = jnp.minimum(sender_start[:, :, None] + slot_grid, LLM_ROWS - 1)
    sender_row = sender_perm[jnp.broadcast_to(sender_grid, sender_place.shape), sender_place]
    target = jnp.where(valid, sender_grid * LLM_ROWS + sender_row, owners * LLM_ROWS).reshape(-1)
    slot_value = jnp.broadcast_to(owner_grid * slot_cap + slot_grid, valid.shape).reshape(-1)
    slots = jnp.full((owners * LLM_ROWS,), -1, jnp.int32).at[target].set(slot_value, mode='drop')
    rows = jnp.full((owners * LLM_ROWS,), -1, jnp.int32).at[target].set(owner_row.reshape(-1), mode='drop')
    return (slots, rows)


def build_routes(key):
    slice_keys = jax.random.split(jax.random.fold_in(key, 7), N_CUTS)
    slots, rows = jax.vmap(route_slice)(slice_keys)
    return (slots.reshape(-1), rows.reshape(-1))


def draw_route_slot(key, part):
    return build_routes(key)[0]


def draw_route_row(key, part):
    return build_routes(key)[1]


def level_of(own_key, shape, pieces, least, high):
    factor_of = 1.0
    for position, shards_of in pieces:
        draws = jax.random.uniform(jax.random.fold_in(jax.random.fold_in(own_key, 6), position), (shards_of,), jnp.float32, least / len(pieces), high / len(pieces))
        factor_of = factor_of * jnp.repeat(jnp.exp(draws), shape[position] // shards_of).reshape((-1,) + (1,) * (len(shape) - 1 - position))
    return factor_of


def gaussian(rng, extent, scale, bound, shards=(), kind=jnp.bfloat16):
    drawn = scale * jax.random.normal(rng, extent, jnp.float32)
    if shards:
        drawn = drawn * level_of(rng, extent, shards, -0.22, 0.18)
    return jnp.clip(drawn, -bound, bound).astype(kind)


def setup_inputs(seed: int = 0) -> dict:
    seeds = jax.random.split(jax.random.key(seed), 6)
    llm_grad = gaussian(seeds[0], (N_CUTS * N_DP * LLM_ROWS, F), 1.0, 6.0, ((0, 128),))
    route_slot = draw_route_slot(jax.random.fold_in(seeds[5], 71), 0)
    route_row = draw_route_row(jax.random.fold_in(seeds[5], 71), 0)
    pre_act = gaussian(seeds[3], (N_CUTS * N_DP * IMG, H), 1.0, 6.0, ((0, 128),))
    down_weight = gaussian(seeds[4], (H, F), H ** -0.5, 0.125)
    return dict(llm_grad=llm_grad, route_slot=route_slot, route_row=route_row, pre_act=pre_act, down_weight=down_weight)


def gelu_parts(pre_value):
    normal_cdf = 0.5 * (1.0 + lax.erf(pre_value * 0.7071067811865476))
    normal_pdf = jnp.exp(-0.5 * pre_value * pre_value) * 0.3989422804014327
    return pre_value * normal_cdf, normal_cdf + pre_value * normal_pdf


def reference(llm_grad, route_slot, route_row, pre_act, down_weight):
    slot_cap = 2 * IMG // N_DP
    total_rows = llm_grad.shape[0]
    slice_of = (jnp.arange(total_rows) // (N_DP * LLM_ROWS)).astype(jnp.int32)
    owner = (route_slot // slot_cap).astype(jnp.int32)
    target = jnp.where(route_slot >= 0, slice_of * (N_DP * IMG) + owner * IMG + route_row, N_CUTS * N_DP * IMG).astype(jnp.int32)
    image_grad = jnp.zeros((N_CUTS * N_DP * IMG, F), jnp.bfloat16).at[target].set(llm_grad, mode="drop")
    gelu_value, gelu_slope = gelu_parts(pre_act.astype(jnp.float32))
    hidden = gelu_value.astype(jnp.bfloat16)
    d_hidden = lax.dot_general(image_grad, down_weight, (((1,), (1,)), ((), ())), preferred_element_type=jnp.float32)
    d_pre = (d_hidden * gelu_slope).astype(jnp.bfloat16)
    summed = lax.dot_general(hidden, image_grad, (((0,), (0,)), ((), ())), preferred_element_type=jnp.float32)
    w_grad = summed / (N_CUTS * N_DP)
    return d_pre, w_grad
```

```python
import jax
import jax.numpy as jnp
from jax import lax
from jax.sharding import PartitionSpec as P


def gelu_parts(pre_value):
    normal_cdf = 0.5 * (1.0 + lax.erf(pre_value * 0.7071067811865476))
    normal_pdf = jnp.exp(-0.5 * pre_value * pre_value) * 0.3989422804014327
    return (pre_value * normal_cdf, normal_cdf + pre_value * normal_pdf)


def dot32(a, b, contract):
    return lax.dot_general(a, b, ((contract[0], contract[1]), ((), ())), preferred_element_type=jnp.float32)


def chunks_of(width, parts):
    tiles = width // 128
    edges = [0]
    for part in range(parts):
        edges.append(edges[-1] + 128 * ((tiles + parts - 1 - part) // parts))
    return list(zip(edges[:-1], edges[1:]))


PARTS = 1


def on_device(llm_grad, route_slot, route_row, pre_act, down_weight):
    dp = lax.axis_size("dp")
    chips = dp // 2
    n_cuts = lax.axis_size("cuts")
    img, hid = pre_act.shape
    feat = llm_grad.shape[1]
    half = feat // 2
    cap = 2 * img // dp
    slots = dp * cap
    swap = [(i, i ^ 1) for i in range(dp)]

    natural = jnp.arange(slots, dtype=jnp.int32)
    swapped = (natural // (2 * cap)) * (2 * cap) + (natural % (2 * cap) + cap) % (2 * cap)
    picks = [(order[:, None] == route_slot[None, :]) for order in (natural, swapped)]
    targets = [
        jnp.max(jnp.where(pick, route_row[None, :], -1), axis=1).reshape(chips, 1, 2 * cap)
        for pick in picks
    ]
    landing = lax.all_to_all(
        jnp.concatenate(targets, axis=1).reshape(dp, 2 * cap), "dp", 0, 0, tiled=True
    ).reshape(dp, 2, cap)
    landing = jnp.where(
        landing >= 0, landing + img * jnp.arange(2, dtype=jnp.int32)[None, :, None], -1
    ).reshape(-1)

    gelu_value, gelu_slope = gelu_parts(pre_act.astype(jnp.float32))
    hidden = gelu_value.astype(jnp.bfloat16)
    hidden_both = jnp.concatenate([hidden, lax.ppermute(hidden, "dp", swap)], axis=0)

    place = (jnp.arange(2 * img, dtype=jnp.int32)[:, None] == landing[None, :]).astype(jnp.bfloat16)
    own_halves = []
    other_halves = []
    sums = []
    for start, stop in chunks_of(half, PARTS):
        width = stop - start
        sent = jnp.stack(
            [
                dot32(
                    picks[core].astype(jnp.bfloat16),
                    llm_grad[:, core * half + start : core * half + stop],
                    ((1,), (0,)),
                )
                .astype(jnp.bfloat16)
                .reshape(chips, 2 * cap, width)
                for core in range(2)
            ],
            axis=1,
        ).reshape(dp, 2 * cap, width)
        got = lax.all_to_all(sent, "dp", 0, 0, tiled=True).reshape(dp * 2 * cap, width)
        rows = dot32(place, got, ((1,), (0,))).astype(jnp.bfloat16)
        partial = dot32(hidden_both, rows, ((0,), (0,))).astype(jnp.bfloat16)
        pieces = lax.all_to_all(partial.reshape(dp, hid // dp, width), "dp", 0, 0, tiled=True)
        total = pieces.reshape(chips, 2, hid // dp, width).astype(jnp.float32).sum(axis=0)
        sums.append(total)
        own_halves.append(rows[:img])
        other_halves.append(lax.ppermute(rows[img:], "dp", swap))

    total = jnp.concatenate(sums, axis=2).transpose(1, 0, 2).reshape(hid // dp, feat)
    total = total + lax.ppermute(total, "cuts", [(i, (i + 1) % n_cuts) for i in range(n_cuts)])
    w_grad = total * (1.0 / (n_cuts * dp))

    core = lax.axis_index("dp") % 2
    mine = jnp.concatenate(own_halves, axis=1)
    theirs = jnp.concatenate(other_halves, axis=1)
    image_grad = jnp.where(
        core == 0, jnp.concatenate([mine, theirs], axis=1), jnp.concatenate([theirs, mine], axis=1)
    )
    d_hidden = dot32(image_grad, down_weight, ((1,), (1,)))
    d_pre = (d_hidden * gelu_slope).astype(jnp.bfloat16)
    return (d_pre, w_grad)


def solution(mesh):
    placed = (
        P(("cuts", "dp"), None),
        P(("cuts", "dp")),
        P(("cuts", "dp")),
        P(("cuts", "dp"), None),
        P(),
    )
    return jax.shard_map(
        on_device,
        mesh=mesh,
        in_specs=placed,
        out_specs=(P(("cuts", "dp"), None), P("dp", None)),
        check_vma=False,
    )
```

```python
import functools

import jax
import jax.numpy as jnp
from jax import lax
from jax.experimental import pallas as pl
from jax.experimental.pallas import tpu as pltpu
from jax.sharding import PartitionSpec as P

BF16 = jnp.bfloat16
F32 = jnp.float32
VMEM_LIMIT = 48 * 1024 * 1024


def gelu_parts(pre_value):
    normal_cdf = 0.5 * (1.0 + lax.erf(pre_value * 0.7071067811865476))
    normal_pdf = jnp.exp(-0.5 * pre_value * pre_value) * 0.3989422804014327
    return (pre_value * normal_cdf, normal_cdf + pre_value * normal_pdf)


def dot32(a, b, contract=((1,), (0,))):
    return lax.dot_general(a, b, (contract, ((), ())), preferred_element_type=F32)


def gather_kernel(block, third, slot_ref, grad_ref, sent_ref, pick_ref):
    side, tile = pl.program_id(0), pl.program_id(1)
    chips = block // (6 * third)

    @pl.when(side == 0)
    def _():
        row = lax.broadcasted_iota(jnp.int32, (block, 1), 0) + tile * block
        place = lax.rem(row, 6 * third)
        slot = row - place + jnp.where(
            place < 3 * third, place, jnp.where(place < 4 * third, place + 2 * third, place - third)
        )
        pick_ref[tile] = jnp.where(slot == slot_ref[...], 1.0, 0.0).astype(BF16)

    rows = dot32(pick_ref[tile], grad_ref[...]).astype(BF16)
    sent_ref[...] = rows.reshape(chips, 1, 6 * third, rows.shape[1])


def gather_rows(llm_grad, route_slot, dp, cap):
    rows, feat = llm_grad.shape
    half = feat // 2
    slots = dp * cap
    chips = dp // 2
    steps = 4
    block = slots // steps
    return pl.pallas_call(
        functools.partial(gather_kernel, block, cap // 3),
        grid=(2, steps),
        in_specs=[
            pl.BlockSpec((1, rows), lambda c, m: (0, 0)),
            pl.BlockSpec((rows, half), lambda c, m: (0, c)),
        ],
        out_specs=pl.BlockSpec((chips // steps, 1, 2 * cap, half), lambda c, m: (m, c, 0, 0)),
        out_shape=pltpu.HBM((chips, 2, 2 * cap, half), BF16),
        scratch_shapes=[pltpu.VMEM((steps, block, rows), BF16)],
        compiler_params=pltpu.CompilerParams(vmem_limit_bytes=VMEM_LIMIT),
        cost_estimate=pl.CostEstimate(
            flops=2 * slots * rows * feat, bytes_accessed=2 * (rows + slots) * feat, transcendentals=0
        ),
        name="gather_rows",
    )(route_slot.reshape(1, rows), llm_grad)


def land_kernel(img, got_ref, land_ref, out_ref, acc_ref):
    step = pl.program_id(0)
    senders = got_ref.shape[0]
    width = got_ref.shape[2]
    span = 2 * got_ref.shape[1] // 3
    row = lax.broadcasted_iota(jnp.int32, (img, 1), 0)
    for owner in range(2):
        place = jnp.where(row == land_ref[owner, 0], 1.0, 0.0).astype(BF16)
        begin = owner * (got_ref.shape[1] - span)
        rows = got_ref[:, begin : begin + span, :].reshape(senders * span, width)
        part = dot32(place, rows)

        @pl.when(step == 0)
        def _():
            acc_ref[owner] = part

        @pl.when(step > 0)
        def _():
            acc_ref[owner] += part

    @pl.when(step == pl.num_programs(0) - 1)
    def _():
        out_ref[...] = acc_ref[...].astype(BF16)


def land_rows(got, landing, img):
    dp, block, half = got.shape
    steps = 4
    span = 2 * block // 3
    return pl.pallas_call(
        functools.partial(land_kernel, img),
        grid=(steps,),
        in_specs=[
            pl.BlockSpec((dp // steps, block, half), lambda k: (k, 0, 0)),
            pl.BlockSpec((2, 1, 1, dp // steps * span), lambda k: (0, k, 0, 0)),
        ],
        out_specs=pl.BlockSpec((2, img, half), lambda k: (0, 0, 0)),
        out_shape=jax.ShapeDtypeStruct((2, img, half), BF16),
        scratch_shapes=[pltpu.VMEM((2, img, half), F32)],
        compiler_params=pltpu.CompilerParams(vmem_limit_bytes=VMEM_LIMIT),
        cost_estimate=pl.CostEstimate(
            flops=4 * img * dp * span * half, bytes_accessed=2 * half * (dp * block + 2 * img), transcendentals=0
        ),
        name="land_rows",
    )(got, landing.reshape(2, steps, 1, dp // steps * span))


def partial_kernel(place_ref, one_ref, two_ref, grad_ref, first_ref, second_ref, acc_ref):
    del place_ref
    step = pl.program_id(0)
    rows = first_ref.shape[0]
    tokens = grad_ref.shape[1]
    left = jnp.concatenate(
        [one_ref[...].reshape(rows, tokens), two_ref[...].reshape(rows, tokens)], axis=0
    )
    part = dot32(left, grad_ref[0])

    @pl.when(step == 0)
    def _():
        acc_ref[...] = part

    @pl.when(step == 1)
    def _():
        total = acc_ref[...] + part
        first_ref[...] = total[:rows].astype(first_ref.dtype)
        second_ref[...] = total[rows:].astype(second_ref.dtype)


def partial_pieces(hidden_t, grad, place, shift, dtype):
    nx, ny, _, share, both = hidden_t.shape
    _, img, half = grad.shape
    out = [jax.ShapeDtypeStruct((n * share, half), dtype) for n in (ny, nx)]
    whole = [pl.BlockSpec((n * share, half), lambda k, p: (0, 0)) for n in (ny, nx)]
    return pl.pallas_call(
        partial_kernel,
        grid_spec=pltpu.PrefetchScalarGridSpec(
            num_scalar_prefetch=1,
            grid=(2,),
            in_specs=[
                pl.BlockSpec((1, ny, 1, share, img), lambda k, p: (p[0] ^ shift, 0, 0, 0, k)),
                pl.BlockSpec((nx, 1, 1, share, img), lambda k, p: (0, p[1] ^ shift, 1, 0, k)),
                pl.BlockSpec((1, img, half), lambda k, p: (k, 0, 0)),
            ],
            out_specs=whole,
            scratch_shapes=[pltpu.VMEM(((nx + ny) * share, half), F32)],
        ),
        out_shape=out,
        compiler_params=pltpu.CompilerParams(vmem_limit_bytes=VMEM_LIMIT),
        cost_estimate=pl.CostEstimate(
            flops=2 * (nx + ny) * share * both * half,
            bytes_accessed=2 * both * ((nx + ny) * share + half) + 4 * (nx + ny) * share * half,
            transcendentals=0,
        ),
        name=f"partial_pieces_{shift}",
    )(place, hidden_t, hidden_t, grad)


def first_sum_kernel(place_ref, *refs):
    del place_ref
    step = pl.program_id(0)
    for stream in range(2):
        own, one, two, three = refs[4 * stream : 4 * stream + 4]
        outs = refs[8 + 4 * stream : 12 + 4 * stream]
        total = own[...] + one[...].astype(F32) + two[...].astype(F32) + three[...].astype(F32)
        for k in range(4):

            @pl.when(step == k)
            def _(out=outs[k]):
                out[...] = total.astype(out.dtype)


def first_sums(place, firsts, seconds, share):
    half = firsts[0].shape[1]
    by_y = pl.BlockSpec((share, half), lambda k, p: (p[1] ^ k, 0))
    by_x = pl.BlockSpec((share, half), lambda k, p: (p[0] ^ k, 0))
    outs = ([jax.ShapeDtypeStruct((share, half), F32)] + [jax.ShapeDtypeStruct((share, half), BF16)] * 3) * 2
    return pl.pallas_call(
        first_sum_kernel,
        grid_spec=pltpu.PrefetchScalarGridSpec(
            num_scalar_prefetch=1,
            grid=(4,),
            in_specs=[by_y] * 4 + [by_x] * 4,
            out_specs=[pl.BlockSpec((share, half), lambda k, p: (0, 0))] * 8,
        ),
        out_shape=outs,
        compiler_params=pltpu.CompilerParams(vmem_limit_bytes=VMEM_LIMIT),
        cost_estimate=pl.CostEstimate(
            flops=32 * share * half, bytes_accessed=100 * share * half, transcendentals=0
        ),
        name="first_sums",
    )(place, *firsts, *seconds)


def second_sum_kernel(place_ref, *refs):
    ones, twos = refs[:4], refs[4:8]
    keep_ref, send_ref = refs[8:]
    first = ones[0][...] + sum(r[...].astype(F32) for r in ones[1:])
    second = twos[0][...] + sum(r[...].astype(F32) for r in twos[1:])
    low = place_ref[2] == 0
    keep_ref[...] = jnp.where(low, first, second)
    send_ref[...] = jnp.where(low, second, first)


def second_sums(place, firsts, seconds):
    share, half = firsts[0].shape
    vmem = pl.BlockSpec(memory_space=pltpu.VMEM)
    return pl.pallas_call(
        second_sum_kernel,
        in_specs=[pl.BlockSpec(memory_space=pltpu.SMEM)] + [vmem] * 8,
        out_specs=[vmem] * 2,
        out_shape=[jax.ShapeDtypeStruct((share, half), F32)] * 2,
        compiler_params=pltpu.CompilerParams(vmem_limit_bytes=VMEM_LIMIT),
        cost_estimate=pl.CostEstimate(
            flops=8 * share * half, bytes_accessed=28 * share * half, transcendentals=0
        ),
        name="second_sums",
    )(place, *firsts, *seconds)


def on_device(shape, llm_grad, route_slot, route_row, pre_act, down_weight):
    nx, ny, nz = shape
    dp = lax.axis_size("dp")
    n_cuts = lax.axis_size("cuts")
    img, hid = pre_act.shape
    feat = llm_grad.shape[1]
    half = feat // 2
    cap = 2 * img // dp
    third = cap // 3
    share = 2 * hid // dp

    def across(value, mask):
        return lax.ppermute(value, "dp", [(i, i ^ mask) for i in range(dp)])

    core_bit, z_bit, y_bit, x_bit = 1, 2, 2 * nz, 2 * nz * ny
    me = lax.axis_index("dp").astype(jnp.int32)
    core = me % 2
    chip = me // 2
    place = jnp.stack([me // x_bit, me // y_bit % ny, me // z_bit % nz, core]).astype(jnp.int32)

    routes = lax.all_gather(jnp.stack([route_slot, route_row]), "dp")
    sent = gather_rows(llm_grad, route_slot, dp, cap).reshape(dp, 2 * cap, half)
    got = lax.all_to_all(sent, "dp", 0, 0, tiled=True)

    near = routes[:, 0] - chip * (2 * cap)
    slot_range = jnp.arange(2 * cap, dtype=jnp.int32)
    landing = jnp.max(
        jnp.where(near[:, None, :] == slot_range[None, :, None], routes[:, 1][:, None, :], -1), axis=2
    )
    zero = jnp.full((dp, third), -1, jnp.int32)
    landing = jnp.stack(
        [
            jnp.concatenate([landing[:, :cap], zero], axis=1),
            jnp.concatenate([zero, landing[:, cap + 2 * third :], landing[:, cap : cap + 2 * third]], axis=1),
        ]
    )

    gelu_value, gelu_slope = gelu_parts(pre_act.astype(F32))
    hidden_t = gelu_value.astype(BF16).T
    theirs_t = across(hidden_t, core_bit)
    hidden_t = jnp.concatenate(
        [jnp.where(core == 0, hidden_t, theirs_t), jnp.where(core == 0, theirs_t, hidden_t)], axis=1
    ).reshape(nx, ny, nz, share, 2 * img)

    got, hidden_t = lax.optimization_barrier((got, hidden_t))
    grad = land_rows(got, landing, img)

    own_half = jnp.where(core == 0, grad[0], grad[1])
    other_half = across(jnp.where(core == 0, grad[1], grad[0]), core_bit)

    firsts, seconds = [], []
    for shift in (1, 2, 3):
        one, two = partial_pieces(hidden_t, grad, place, shift, BF16)
        firsts.append(across(one, shift * x_bit))
        seconds.append(across(two, shift * y_bit))
    one, two = partial_pieces(hidden_t, grad, place, 0, F32)
    image_grad = jnp.where(
        core == 0,
        jnp.concatenate([own_half, other_half], axis=1),
        jnp.concatenate([other_half, own_half], axis=1),
    )
    d_hidden = dot32(image_grad, down_weight, ((1,), (1,)))
    d_pre = (d_hidden * gelu_slope).astype(BF16)
    one, two, d_pre = lax.optimization_barrier((one, two, d_pre))
    sums = first_sums(place, [one] + firsts, [two] + seconds, share)
    firsts = [sums[0]] + [across(sums[k], k * y_bit) for k in (1, 2, 3)]
    seconds = [sums[4]] + [across(sums[4 + k], k * x_bit) for k in (1, 2, 3)]
    keep, send = second_sums(place, firsts, seconds)

    def over(value, mask, turn):
        pairs = [
            (c * dp + i, ((c + turn) % n_cuts) * dp + (i ^ mask)) for c in range(n_cuts) for i in range(dp)
        ]
        return lax.ppermute(value, ("cuts", "dp"), pairs)

    total = keep + over(send, z_bit, 0)
    for turn in range(1, n_cuts):
        total = total + over(keep, 0, turn) + over(send, z_bit, turn)
    total = (total * (1.0 / (n_cuts * dp))).reshape(2, share // 2, half)
    mine = jnp.where(core == 0, total[0], total[1])
    other = across(jnp.where(core == 0, total[1], total[0]), core_bit)
    w_grad = jnp.concatenate(
        [jnp.where(core == 0, mine, other), jnp.where(core == 0, other, mine)], axis=1
    )

    return (d_pre, w_grad)


def solution(mesh):
    placed = (
        P(("cuts", "dp"), None),
        P(("cuts", "dp")),
        P(("cuts", "dp")),
        P(("cuts", "dp"), None),
        P(),
    )
    return jax.shard_map(
        functools.partial(on_device, (4, 4, 2)),
        mesh=mesh,
        in_specs=placed,
        out_specs=(P(("cuts", "dp"), None), P("dp", None)),
        check_vma=False,
    )
```

```python
import functools

import jax
import jax.numpy as jnp
from jax import lax
from jax.experimental import pallas as pl
from jax.experimental.pallas import tpu as pltpu
from jax.sharding import PartitionSpec as P

BF16 = jnp.bfloat16
F32 = jnp.float32
VMEM_LIMIT = 48 * 1024 * 1024


def gelu_parts(pre_value):
    normal_cdf = 0.5 * (1.0 + lax.erf(pre_value * 0.7071067811865476))
    normal_pdf = jnp.exp(-0.5 * pre_value * pre_value) * 0.3989422804014327
    return (pre_value * normal_cdf, normal_cdf + pre_value * normal_pdf)


def dot32(a, b, contract=((1,), (0,))):
    return lax.dot_general(a, b, (contract, ((), ())), preferred_element_type=F32)


def slot_order(place, third):
    return jnp.where(
        place < 3 * third, place, jnp.where(place < 4 * third, place + 2 * third, place - third)
    )


def gather_kernel(third, slot_ref, note_ref, grad_ref, sent_ref, pick_ref):
    side, part = pl.program_id(0), pl.program_id(1)
    last = pl.num_programs(1) - 1
    first = (side == 0) & (part == 0)
    block = 6 * third
    steps, rows_per = pick_ref.shape[:2]
    chips = rows_per // block

    def emit(step, pick):
        rows = dot32(pick, grad_ref[...]).astype(BF16)
        return rows[:, :128].reshape(chips, block, 128), rows[:, 128:].reshape(chips, block, 128)

    def store(step, low, high):
        chip = pl.ds(step * chips, chips)
        sent_ref[chip, 0, :block] = low
        sent_ref[chip, 0, block:] = high

    @pl.when(first)
    def _():
        for step in range(steps):
            row = lax.broadcasted_iota(jnp.int32, (rows_per, 1), 0) + step * rows_per
            place = lax.rem(row, block)
            slot = row - place + slot_order(place, third)
            pick = jnp.where(slot == slot_ref[...], 1.0, 0.0).astype(BF16)
            pick_ref[step] = pick
            store(step, *emit(step, pick))

    @pl.when(jnp.logical_not(first) & (part < last))
    def _():
        for step in range(steps):
            store(step, *emit(step, pick_ref[step]))

    @pl.when(part == last)
    def _():
        for step in range(steps):
            chip = pl.ds(step * chips, chips)
            sent_ref[chip, 0, :block] = emit(step, pick_ref[step])[1]
            sent_ref[chip, 0, block : block + 16] = note_ref[chip]


def gather_rows(llm_grad, route_slot, notes, dp, cap):
    rows, feat = llm_grad.shape
    half = feat // 2
    slots = dp * cap
    chips = dp // 2
    steps = 8
    return pl.pallas_call(
        functools.partial(gather_kernel, cap // 3),
        grid=(2, pl.cdiv(half, 256)),
        in_specs=[
            pl.BlockSpec((1, rows), lambda c, n: (0, 0)),
            pl.BlockSpec((chips, 16, 128), lambda c, n: (0, 0, 0)),
            pl.BlockSpec(
                (pl.Element(rows), pl.Element(256)),
                lambda c, n: (0, pl.multiple_of(c * half + jnp.minimum(n * 256, half - 256), 128)),
            ),
        ],
        out_specs=pl.BlockSpec((chips, 1, 4 * cap, 128), lambda c, n: (0, c, n, 0)),
        out_shape=pltpu.HBM((chips, 2, half // 128 * 2 * cap + 16, 128), BF16),
        scratch_shapes=[pltpu.VMEM((steps, slots // steps, rows), BF16)],
        compiler_params=pltpu.CompilerParams(vmem_limit_bytes=VMEM_LIMIT),
        cost_estimate=pl.CostEstimate(
            flops=2 * slots * rows * feat, bytes_accessed=2 * (rows + slots) * feat, transcendentals=0
        ),
        name="gather_rows",
    )(route_slot.reshape(1, rows), notes, llm_grad)


def land_kernel(place_ref, got_ref, land_ref, mine_ref, theirs_ref, pick_ref):
    part = pl.program_id(0)
    last = pl.num_programs(0) - 1
    senders, both, _ = got_ref.shape
    block = both // 2
    span = 2 * block // 3
    img = mine_ref.shape[0]
    outs = (mine_ref, theirs_ref)

    @pl.when(part == 0)
    def _():
        row = lax.broadcasted_iota(jnp.int32, (img, 1), 0)
        for side in range(2):
            pick_ref[side] = jnp.where(row == land_ref[side ^ place_ref[3]], 1.0, 0.0).astype(BF16)

    def rows(side, tile):
        begin = pl.multiple_of((side ^ place_ref[3]) * (block - span) + tile * block, 16)
        return got_ref[:, pl.ds(begin, span), :].reshape(senders * span, 128)

    for side in range(2):

        @pl.when(part < last)
        def _(side=side):
            right = jnp.concatenate([rows(side, 0), rows(side, 1)], axis=1)
            outs[side][...] = dot32(pick_ref[side], right).astype(BF16)

        @pl.when(part == last)
        def _(side=side):
            outs[side][:, :128] = dot32(pick_ref[side], rows(side, 0)).astype(BF16)


def land_rows(place, got, landing, img, half, cap):
    dp = got.shape[0]
    span = 4 * cap // 3
    return pl.pallas_call(
        land_kernel,
        grid_spec=pltpu.PrefetchScalarGridSpec(
            num_scalar_prefetch=1,
            grid=(pl.cdiv(half, 256),),
            in_specs=[
                pl.BlockSpec((dp, 4 * cap, 128), lambda n, p: (0, n, 0)),
                pl.BlockSpec((2, 1, dp * span), lambda n, p: (0, 0, 0)),
            ],
            out_specs=[pl.BlockSpec((img, 256), lambda n, p: (0, n))] * 2,
            scratch_shapes=[pltpu.VMEM((2, img, dp * span), BF16)],
        ),
        out_shape=[jax.ShapeDtypeStruct((img, half), BF16)] * 2,
        compiler_params=pltpu.CompilerParams(vmem_limit_bytes=VMEM_LIMIT),
        cost_estimate=pl.CostEstimate(
            flops=4 * img * dp * span * half, bytes_accessed=4 * half * (dp * cap + img), transcendentals=0
        ),
        name="land_rows",
    )(place, got, landing.reshape(2, 1, dp * span))


def hidden_kernel(pre_ref, out_ref, *slope_ref):
    value, slope = gelu_parts(pre_ref[...].astype(F32))
    out_ref[...] = value.T.astype(BF16)
    if slope_ref:
        slope_ref[0][...] = slope


def hidden_transposed(pre_act, with_slope):
    img, hid = pre_act.shape
    out = [(pl.BlockSpec((256, img), lambda n: (n, 0)), jax.ShapeDtypeStruct((hid, img), BF16))]
    if with_slope:
        out.append((pl.BlockSpec((img, 256), lambda n: (0, n)), pltpu.HBM((img, hid), F32)))
    return pl.pallas_call(
        hidden_kernel,
        grid=(hid // 256,),
        in_specs=[pl.BlockSpec((img, 256), lambda n: (0, n))],
        out_specs=[spec for spec, _ in out],
        out_shape=[kind for _, kind in out],
        compiler_params=pltpu.CompilerParams(vmem_limit_bytes=VMEM_LIMIT),
        cost_estimate=pl.CostEstimate(
            flops=30 * img * hid, bytes_accessed=4 * img * hid, transcendentals=img * hid
        ),
        name="hidden_transposed",
    )(pre_act)


def d_pre_kernel(place_ref, mine_ref, theirs_ref, near_ref, far_ref, slope_ref, *rest):
    del place_ref
    out_ref = rest[-1]
    contract = ((1,), (1,))
    total = dot32(mine_ref[...], near_ref[...], contract) + dot32(theirs_ref[...], far_ref[...], contract)
    out_ref[...] = (total * slope_ref[...]).astype(BF16)


def d_pre_columns(place, mine, theirs, weight, slope, begin, count, before=None):
    img, half = mine.shape
    hid = weight.shape[0]
    in_specs = [
        pl.BlockSpec((img, half), lambda n, p: (0, 0)),
        pl.BlockSpec((img, half), lambda n, p: (0, 0)),
        pl.BlockSpec((256, half), lambda n, p: (n + begin, p[3])),
        pl.BlockSpec((256, half), lambda n, p: (n + begin, 1 - p[3])),
        pl.BlockSpec((img, 256), lambda n, p: (0, n + begin)),
    ]
    operands = [place, mine, theirs, weight, weight, slope]
    aliases = {}
    if before is not None:
        in_specs.append(pl.BlockSpec(memory_space=pl.ANY))
        aliases = {len(operands): 0}
        operands.append(before)
    return pl.pallas_call(
        d_pre_kernel,
        grid_spec=pltpu.PrefetchScalarGridSpec(
            num_scalar_prefetch=1,
            grid=(count,),
            in_specs=in_specs,
            out_specs=pl.BlockSpec((img, 256), lambda n, p: (0, n + begin)),
        ),
        out_shape=pltpu.HBM((img, hid), BF16),
        input_output_aliases=aliases,
        compiler_params=pltpu.CompilerParams(vmem_limit_bytes=VMEM_LIMIT),
        cost_estimate=pl.CostEstimate(
            flops=4 * img * half * 256 * count,
            bytes_accessed=256 * count * (4 * half + 6 * img) + 4 * img * half,
            transcendentals=0,
        ),
        name=f"d_pre_{begin}",
    )(*operands)


def partial_kernel(place_ref, *refs):
    del place_ref
    step = pl.program_id(0)
    lefts, grads, outs = refs[:4], refs[4:6], refs[6:]
    for stream in range(2):
        for number in range(len(outs) // 2):
            out = outs[2 * number + stream]

            @pl.when(step == number)
            def _(out=out, stream=stream):
                rows = out.shape[0]
                one, two = (lefts[2 * stream + side][...].reshape(rows, -1) for side in range(2))
                total = dot32(one, grads[0][...]) + dot32(two, grads[1][...])
                out[...] = total.astype(out.dtype)


def partial_pieces(mine_t, theirs_t, grads, place, shifts):
    nx, ny, _, share, img = mine_t.shape
    half = grads[0].shape[1]
    table = jnp.concatenate([place, jnp.array(shifts, jnp.int32)])
    by_x = pl.BlockSpec((1, ny, 1, share, img), lambda k, p: (p[0] ^ p[4 + k], 0, 0, 0, 0))
    by_y = pl.BlockSpec((nx, 1, 1, share, img), lambda k, p: (0, p[1] ^ p[4 + k], 1, 0, 0))
    whole = pl.BlockSpec((img, half), lambda k, p: (0, 0))
    sizes = [(n * share, half) for n in (ny, nx)]
    return pl.pallas_call(
        partial_kernel,
        grid_spec=pltpu.PrefetchScalarGridSpec(
            num_scalar_prefetch=1,
            grid=(len(shifts),),
            in_specs=[by_x, by_x, by_y, by_y, whole, whole],
            out_specs=[pl.BlockSpec(size, lambda k, p: (0, 0)) for size in sizes * len(shifts)],
        ),
        out_shape=[jax.ShapeDtypeStruct(size, BF16 if shift else F32) for shift in shifts for size in sizes],
        compiler_params=pltpu.CompilerParams(vmem_limit_bytes=VMEM_LIMIT),
        cost_estimate=pl.CostEstimate(
            flops=4 * (nx + ny) * share * img * half * len(shifts),
            bytes_accessed=4 * img * ((nx + ny) * share * len(shifts) + half),
            transcendentals=0,
        ),
        name=f"partial_pieces_{len(shifts)}",
    )(table, mine_t, theirs_t, mine_t, theirs_t, *grads)


def first_sum_kernel(place_ref, *refs):
    del place_ref
    step = pl.program_id(0)
    for stream in range(2):
        own, one, two, three = refs[4 * stream : 4 * stream + 4]
        outs = refs[8 + 4 * stream : 12 + 4 * stream]
        total = own[...] + one[...].astype(F32) + two[...].astype(F32) + three[...].astype(F32)
        for k in range(4):

            @pl.when(step == k)
            def _(out=outs[k]):
                out[...] = total.astype(out.dtype)


def first_sums(place, firsts, seconds, share):
    half = firsts[0].shape[1]
    by_y = pl.BlockSpec((share, half), lambda k, p: (p[1] ^ k, 0))
    by_x = pl.BlockSpec((share, half), lambda k, p: (p[0] ^ k, 0))
    outs = ([jax.ShapeDtypeStruct((share, half), F32)] + [jax.ShapeDtypeStruct((share, half), BF16)] * 3) * 2
    return pl.pallas_call(
        first_sum_kernel,
        grid_spec=pltpu.PrefetchScalarGridSpec(
            num_scalar_prefetch=1,
            grid=(4,),
            in_specs=[by_y] * 4 + [by_x] * 4,
            out_specs=[pl.BlockSpec((share, half), lambda k, p: (0, 0))] * 8,
        ),
        out_shape=outs,
        compiler_params=pltpu.CompilerParams(vmem_limit_bytes=VMEM_LIMIT),
        cost_estimate=pl.CostEstimate(
            flops=32 * share * half, bytes_accessed=100 * share * half, transcendentals=0
        ),
        name="first_sums",
    )(place, *firsts, *seconds)


def second_sum_kernel(place_ref, *refs):
    ones, twos = refs[:4], refs[4:8]
    own_ref, keep_ref, send_ref = refs[8:]
    first = ones[0][...] + sum(r[...].astype(F32) for r in ones[1:])
    second = twos[0][...] + sum(r[...].astype(F32) for r in twos[1:])
    low = place_ref[2] == 0
    own = jnp.where(low, first, second)
    own_ref[...] = own
    keep_ref[...] = own.astype(BF16)
    send_ref[...] = jnp.where(low, second, first).astype(BF16)


def second_sums(place, firsts, seconds):
    share, half = firsts[0].shape
    vmem = pl.BlockSpec(memory_space=pltpu.VMEM)
    return pl.pallas_call(
        second_sum_kernel,
        in_specs=[pl.BlockSpec(memory_space=pltpu.SMEM)] + [vmem] * 8,
        out_specs=[vmem] * 3,
        out_shape=[jax.ShapeDtypeStruct((share, half), kind) for kind in (F32, BF16, BF16)],
        compiler_params=pltpu.CompilerParams(vmem_limit_bytes=VMEM_LIMIT),
        cost_estimate=pl.CostEstimate(
            flops=8 * share * half, bytes_accessed=28 * share * half, transcendentals=0
        ),
        name="second_sums",
    )(place, *firsts, *seconds)


def on_device(shape, llm_grad, route_slot, route_row, pre_act, down_weight):
    nx, ny, nz = shape
    dp = lax.axis_size("dp")
    n_cuts = lax.axis_size("cuts")
    img, hid = pre_act.shape
    half = llm_grad.shape[1] // 2
    cap = 2 * img // dp
    third = cap // 3
    share = 2 * hid // dp
    core_bit, z_bit, y_bit, x_bit = 1, 2, 2 * nz, 2 * nz * ny

    def across(value, mask):
        return lax.ppermute(value, "dp", [(i, i ^ mask) for i in range(dp)])

    def over(value, mask, turn):
        pairs = [
            (c * dp + i, ((c + turn) % n_cuts) * dp + (i ^ mask)) for c in range(n_cuts) for i in range(dp)
        ]
        return lax.ppermute(value, ("cuts", "dp"), pairs)

    me = lax.axis_index("dp").astype(jnp.int32)
    x, y, z, core = me // x_bit, me // y_bit % ny, me // z_bit % nz, me % 2
    place = jnp.stack([x, y, z, core]).astype(jnp.int32)

    their_pre = across(pre_act, core_bit)

    slots = jnp.arange(dp * cap, dtype=jnp.int32)
    slots = slots - slots % (2 * cap) + slot_order(slots % (2 * cap), third)
    number = jnp.max(jnp.where(slots[:, None] == route_slot[None, :], route_row[None, :], -1), axis=1)
    number = number.reshape(dp // 2, 1, 2 * cap)
    notes = jnp.concatenate([number // 32, number % 32], axis=1).astype(BF16)
    notes = jnp.pad(notes, ((0, 0), (0, 14), (0, 128 - 2 * cap)))

    sent = gather_rows(llm_grad, route_slot, notes, dp, cap)
    sent = sent.reshape(dp, sent.shape[2], 128)
    sent, pre_act, their_pre = lax.optimization_barrier((sent, pre_act, their_pre))
    got = lax.all_to_all(sent, "dp", 0, 0, tiled=True)

    mine_t, slope = hidden_transposed(pre_act, True)
    (theirs_t,) = hidden_transposed(their_pre, False)
    got, mine_t, theirs_t, slope, place = lax.optimization_barrier((got, mine_t, theirs_t, slope, place))
    mine_t = mine_t.reshape(nx, ny, nz, share, img)
    theirs_t = theirs_t.reshape(nx, ny, nz, share, img)

    notes = got[:, half // 128 * 2 * cap :][:, :2, : 2 * cap].astype(jnp.int32)
    landing = notes[:, 0] * 32 + notes[:, 1]
    landing = jnp.where(landing >= 0, landing, -1)
    lane = jnp.arange(4 * third, dtype=jnp.int32)
    landing = jnp.stack(
        [
            jnp.where(lane < cap, landing[:, : 4 * third], -1),
            jnp.where(lane >= third, landing[:, 2 * third :], -1),
        ]
    )
    grads = land_rows(place, got, landing, img, half, cap)

    firsts, seconds = {}, {}
    for shifts in ((2,), (1, 3, 0)):
        pieces = partial_pieces(mine_t, theirs_t, grads, place, shifts)
        for k, shift in enumerate(shifts):
            one, two = pieces[2 * k : 2 * k + 2]
            firsts[shift] = across(one, shift * x_bit) if shift else one
            seconds[shift] = across(two, shift * y_bit) if shift else two

    blocks = hid // 256
    early = blocks // 2
    others = across(grads[1], core_bit)
    d_pre = d_pre_columns(place, grads[0], others, down_weight, slope, 0, early)
    firsts[0], seconds[0], d_pre = lax.optimization_barrier((firsts[0], seconds[0], d_pre))

    sums = first_sums(place, [firsts[k] for k in range(4)], [seconds[k] for k in range(4)], share)
    firsts = [sums[0]] + [across(sums[k], k * y_bit) for k in (1, 2, 3)]
    seconds = [sums[4]] + [across(sums[4 + k], k * x_bit) for k in (1, 2, 3)]
    total, keep, send = second_sums(place, firsts, seconds)

    d_pre, keep, send, total = lax.optimization_barrier((d_pre, keep, send, total))
    d_pre = d_pre_columns(place, grads[0], others, down_weight, slope, early, blocks - early, d_pre)
    total, d_pre = lax.optimization_barrier((total, d_pre))
    total = total + over(send, z_bit, 0).astype(F32)
    for turn in range(1, n_cuts):
        total = total + over(keep, 0, turn).astype(F32) + over(send, z_bit, turn).astype(F32)

    total = (total * (1.0 / (n_cuts * dp))).reshape(2, share // 2, half)
    mine = jnp.where(core == 0, total[0], total[1])
    other = across(jnp.where(core == 0, total[1], total[0]), core_bit)
    w_grad = jnp.concatenate([jnp.where(core == 0, mine, other), jnp.where(core == 0, other, mine)], axis=1)
    return (d_pre, w_grad)


def solution(mesh):
    placed = (
        P(("cuts", "dp"), None),
        P(("cuts", "dp")),
        P(("cuts", "dp")),
        P(("cuts", "dp"), None),
        P(),
    )
    return jax.shard_map(
        functools.partial(on_device, (4, 4, 2)),
        mesh=mesh,
        in_specs=placed,
        out_specs=(P(("cuts", "dp"), None), P("dp", None)),
        check_vma=False,
    )
```

```python
import functools

import jax
import jax.numpy as jnp
from jax import lax
from jax.experimental import pallas as pl
from jax.experimental.pallas import tpu as pltpu
from jax.sharding import PartitionSpec as P

BF16 = jnp.bfloat16
VMEM = pl.BlockSpec(memory_space=pltpu.VMEM)
SMEM = pl.BlockSpec(memory_space=pltpu.SMEM)
F32 = jnp.float32
VMEM_LIMIT = 28 * 1024 * 1024
VMEM_LARGE = 54 * 1024 * 1024
VMEM_DPRE = 50 * 1024 * 1024


def gelu_parts(pre_value):
    normal_cdf = 0.5 * (1.0 + lax.erf(pre_value * 0.7071067811865476))
    normal_pdf = jnp.exp(-0.5 * pre_value * pre_value) * 0.3989422804014327
    return (pre_value * normal_cdf, normal_cdf + pre_value * normal_pdf)


def dot32(a, b, contract=((1,), (0,))):
    return lax.dot_general(a, b, (contract, ((), ())), preferred_element_type=F32)


def slot_order(place, third):
    return jnp.where(
        place < 3 * third, place, jnp.where(place < 4 * third, place + 2 * third, place - third)
    )


def gather_kernel(third, slot_ref, note_ref, grad_ref, sent_ref, pick_ref):
    side, part = pl.program_id(0), pl.program_id(1)
    last = pl.num_programs(1) - 1
    first = (side == 0) & (part == 0)
    block = 6 * third
    steps, rows_per = pick_ref.shape[:2]
    chips = rows_per // block

    def emit(step, pick):
        rows = dot32(pick, grad_ref[...]).astype(BF16)
        return rows[:, :128].reshape(chips, block, 128), rows[:, 128:].reshape(chips, block, 128)

    def store(step, low, high):
        chip = pl.ds(step * chips, chips)
        sent_ref[chip, 0, :block] = low
        sent_ref[chip, 0, block:] = high

    @pl.when(first)
    def _():
        for step in range(steps):
            row = lax.broadcasted_iota(jnp.int32, (rows_per, 1), 0) + step * rows_per
            place = lax.rem(row, block)
            slot = row - place + slot_order(place, third)
            pick = jnp.where(slot == slot_ref[...], 1.0, 0.0).astype(BF16)
            pick_ref[step] = pick
            store(step, *emit(step, pick))

    @pl.when(jnp.logical_not(first) & (part < last))
    def _():
        for step in range(steps):
            store(step, *emit(step, pick_ref[step]))

    @pl.when(part == last)
    def _():
        for step in range(steps):
            chip = pl.ds(step * chips, chips)
            sent_ref[chip, 0, :block] = emit(step, pick_ref[step])[1]
            sent_ref[chip, 0, block : block + 16] = note_ref[chip]


def gather_rows(llm_grad, route_slot, notes, dp, cap):
    rows, feat = llm_grad.shape
    half = feat // 2
    slots = dp * cap
    chips = dp // 2
    steps = 8
    return pl.pallas_call(
        functools.partial(gather_kernel, cap // 3),
        grid=(2, pl.cdiv(half, 256)),
        in_specs=[
            pl.BlockSpec((1, rows), lambda c, n: (0, 0)),
            pl.BlockSpec((chips, 16, 128), lambda c, n: (0, 0, 0)),
            pl.BlockSpec(
                (pl.Element(rows), pl.Element(256)),
                lambda c, n: (0, pl.multiple_of(c * half + jnp.minimum(n * 256, half - 256), 128)),
            ),
        ],
        out_specs=pl.BlockSpec((chips, 1, 4 * cap, 128), lambda c, n: (0, c, n, 0)),
        out_shape=pltpu.HBM((chips, 2, half // 128 * 2 * cap + 16, 128), BF16),
        scratch_shapes=[pltpu.VMEM((steps, slots // steps, rows), BF16)],
        compiler_params=pltpu.CompilerParams(vmem_limit_bytes=VMEM_LARGE),
        cost_estimate=pl.CostEstimate(
            flops=2 * slots * rows * feat, bytes_accessed=2 * (rows + slots) * feat, transcendentals=0
        ),
        name="gather_rows",
    )(route_slot.reshape(1, rows), notes, llm_grad)


def land_kernel(place_ref, got_ref, land_ref, mine_ref, theirs_ref, pick_ref):
    part = pl.program_id(0)
    last = pl.num_programs(0) - 1
    senders, both, _ = got_ref.shape
    block = both // 2
    span = 2 * block // 3
    img = mine_ref.shape[0]
    outs = (mine_ref, theirs_ref)

    @pl.when(part == 0)
    def _():
        row = lax.broadcasted_iota(jnp.int32, (img, 1), 0)
        for side in range(2):
            pick_ref[side] = jnp.where(row == land_ref[side ^ place_ref[3]], 1.0, 0.0).astype(BF16)

    def rows(side, tile):
        begin = pl.multiple_of((side ^ place_ref[3]) * (block - span) + tile * block, 16)
        return got_ref[:, pl.ds(begin, span), :].reshape(senders * span, 128)

    for side in range(2):

        @pl.when(part < last)
        def _(side=side):
            right = jnp.concatenate([rows(side, 0), rows(side, 1)], axis=1)
            outs[side][...] = dot32(pick_ref[side], right).astype(BF16)

        @pl.when(part == last)
        def _(side=side):
            outs[side][:, :128] = dot32(pick_ref[side], rows(side, 0)).astype(BF16)


def land_rows(place, got, landing, img, half, cap):
    dp = got.shape[0]
    span = 4 * cap // 3
    return pl.pallas_call(
        land_kernel,
        grid_spec=pltpu.PrefetchScalarGridSpec(
            num_scalar_prefetch=1,
            grid=(pl.cdiv(half, 256),),
            in_specs=[
                pl.BlockSpec((dp, 4 * cap, 128), lambda n, p: (0, n, 0)),
                pl.BlockSpec((2, 1, dp * span), lambda n, p: (0, 0, 0)),
            ],
            out_specs=[pl.BlockSpec((img, 256), lambda n, p: (0, n))] * 2,
            scratch_shapes=[pltpu.VMEM((2, img, dp * span), BF16)],
        ),
        out_shape=[jax.ShapeDtypeStruct((img, half), BF16)] * 2,
        compiler_params=pltpu.CompilerParams(vmem_limit_bytes=VMEM_LIMIT),
        cost_estimate=pl.CostEstimate(
            flops=4 * img * dp * span * half, bytes_accessed=4 * half * (dp * cap + img), transcendentals=0
        ),
        name="land_rows",
    )(place, got, landing.reshape(2, 1, dp * span))


def hidden_kernel(pre_ref, out_ref, *slope_ref):
    value, slope = gelu_parts(pre_ref[...].astype(F32))
    out_ref[...] = value.T.astype(BF16)
    if slope_ref:
        slope_ref[0][...] = slope


def hidden_transposed(pre_act, with_slope):
    img, hid = pre_act.shape
    out = [(pl.BlockSpec((256, img), lambda n: (n, 0)), jax.ShapeDtypeStruct((hid, img), BF16))]
    if with_slope:
        out.append((pl.BlockSpec((img, 256), lambda n: (0, n)), pltpu.HBM((img, hid), F32)))
    return pl.pallas_call(
        hidden_kernel,
        grid=(hid // 256,),
        in_specs=[pl.BlockSpec((img, 256), lambda n: (0, n))],
        out_specs=[spec for spec, _ in out],
        out_shape=[kind for _, kind in out],
        compiler_params=pltpu.CompilerParams(vmem_limit_bytes=VMEM_LIMIT),
        cost_estimate=pl.CostEstimate(
            flops=30 * img * hid, bytes_accessed=4 * img * hid, transcendentals=img * hid
        ),
        name="hidden_transposed",
    )(pre_act)


def d_pre_kernel(place_ref, mine_ref, theirs_ref, weight_ref, slope_ref, out_ref, both_ref):
    half = mine_ref.shape[1]

    @pl.when(pl.program_id(0) == 0)
    def _():
        core = place_ref[3]
        both_ref[:, pl.ds(pl.multiple_of(core * half, 128), half)] = mine_ref[...]
        both_ref[:, pl.ds(pl.multiple_of((1 - core) * half, 128), half)] = theirs_ref[...]

    out_ref[...] = (dot32(both_ref[...], weight_ref[...]) * slope_ref[...]).astype(BF16)


def d_pre_product(place, mine, theirs, weight_t, slope):
    img, half = mine.shape
    hid = weight_t.shape[1]
    return pl.pallas_call(
        d_pre_kernel,
        grid_spec=pltpu.PrefetchScalarGridSpec(
            num_scalar_prefetch=1,
            grid=(hid // 256,),
            in_specs=[
                VMEM,
                VMEM,
                pl.BlockSpec((2 * half, 256), lambda n, p: (0, n)),
                pl.BlockSpec((img, 256), lambda n, p: (0, n)),
            ],
            out_specs=pl.BlockSpec((img, 256), lambda n, p: (0, n)),
            scratch_shapes=[pltpu.VMEM((img, 2 * half), BF16)],
        ),
        out_shape=pltpu.HBM((img, hid), BF16),
        compiler_params=pltpu.CompilerParams(vmem_limit_bytes=VMEM_DPRE),
        cost_estimate=pl.CostEstimate(
            flops=4 * img * half * hid, bytes_accessed=4 * hid * half + 6 * img * hid, transcendentals=0
        ),
        name="d_pre",
    )(place, mine, theirs, weight_t, slope)


def partial_kernel(shift, place_ref, mine_ref, theirs_ref, near_ref, far_ref, first_ref, second_ref):
    img = near_ref.shape[0]
    for stream, out in enumerate((first_ref, second_ref)):
        at = place_ref[stream] ^ shift
        total = 0.0
        for left, grad in ((mine_ref, near_ref), (theirs_ref, far_ref)):
            block = left[:, at, 1] if stream else left[at, :, 0]
            total = total + dot32(block.reshape(out.shape[0], img), grad[...])
        out[...] = total.astype(out.dtype)


def partial_pieces(mine_t, theirs_t, grads, place, shift):
    nx, ny, _, share, img = mine_t.shape
    half = grads[0].shape[1]
    return pl.pallas_call(
        functools.partial(partial_kernel, shift),
        in_specs=[SMEM] + [VMEM] * 4,
        out_specs=[VMEM] * 2,
        out_shape=[jax.ShapeDtypeStruct((n * share, half), BF16 if shift else F32) for n in (ny, nx)],
        compiler_params=pltpu.CompilerParams(vmem_limit_bytes=VMEM_LIMIT),
        cost_estimate=pl.CostEstimate(
            flops=4 * (nx + ny) * share * img * half,
            bytes_accessed=4 * img * ((nx + ny) * share + half),
            transcendentals=0,
        ),
        name=f"partial_pieces_{shift}",
    )(place, mine_t, theirs_t, *grads)


def first_sum_kernel(place_ref, *refs):
    for stream in range(2):
        own, one, two, three = refs[4 * stream : 4 * stream + 4]
        for k, out in enumerate(refs[8 + 4 * stream : 12 + 4 * stream]):
            share = out.shape[0]
            rows = pl.ds(pl.multiple_of((place_ref[1 - stream] ^ k) * share, 16), share)
            total = own[rows] + one[rows].astype(F32) + two[rows].astype(F32) + three[rows].astype(F32)
            out[...] = total.astype(out.dtype)


def first_sums(place, firsts, seconds, share):
    half = firsts[0].shape[1]
    outs = ([jax.ShapeDtypeStruct((share, half), F32)] + [jax.ShapeDtypeStruct((share, half), BF16)] * 3) * 2
    return pl.pallas_call(
        first_sum_kernel,
        in_specs=[SMEM] + [VMEM] * 8,
        out_specs=[VMEM] * 8,
        out_shape=outs,
        compiler_params=pltpu.CompilerParams(vmem_limit_bytes=VMEM_LIMIT),
        cost_estimate=pl.CostEstimate(
            flops=32 * share * half, bytes_accessed=100 * share * half, transcendentals=0
        ),
        name="first_sums",
    )(place, *firsts, *seconds)


def second_sum_kernel(place_ref, *refs):
    ones, twos = refs[:4], refs[4:8]
    own_ref, keep_ref, send_ref = refs[8:]
    first = ones[0][...] + sum(r[...].astype(F32) for r in ones[1:])
    second = twos[0][...] + sum(r[...].astype(F32) for r in twos[1:])
    low = place_ref[2] == 0
    own = jnp.where(low, first, second)
    own_ref[...] = own
    keep_ref[...] = own.astype(BF16)
    send_ref[...] = jnp.where(low, second, first).astype(BF16)


def second_sums(place, firsts, seconds):
    share, half = firsts[0].shape
    vmem = pl.BlockSpec(memory_space=pltpu.VMEM)
    return pl.pallas_call(
        second_sum_kernel,
        in_specs=[pl.BlockSpec(memory_space=pltpu.SMEM)] + [vmem] * 8,
        out_specs=[vmem] * 3,
        out_shape=[jax.ShapeDtypeStruct((share, half), kind) for kind in (F32, BF16, BF16)],
        compiler_params=pltpu.CompilerParams(vmem_limit_bytes=VMEM_LIMIT),
        cost_estimate=pl.CostEstimate(
            flops=8 * share * half, bytes_accessed=28 * share * half, transcendentals=0
        ),
        name="second_sums",
    )(place, *firsts, *seconds)


def on_device(shape, llm_grad, route_slot, route_row, pre_act, down_weight):
    nx, ny, nz = shape
    dp = lax.axis_size("dp")
    n_cuts = lax.axis_size("cuts")
    img, hid = pre_act.shape
    half = llm_grad.shape[1] // 2
    cap = 2 * img // dp
    third = cap // 3
    share = 2 * hid // dp
    core_bit, z_bit, y_bit, x_bit = 1, 2, 2 * nz, 2 * nz * ny

    def across(value, mask):
        return lax.ppermute(value, "dp", [(i, i ^ mask) for i in range(dp)])

    def over(value, mask, turn):
        pairs = [
            (c * dp + i, ((c + turn) % n_cuts) * dp + (i ^ mask)) for c in range(n_cuts) for i in range(dp)
        ]
        return lax.ppermute(value, ("cuts", "dp"), pairs)

    me = lax.axis_index("dp").astype(jnp.int32)
    x, y, z, core = me // x_bit, me // y_bit % ny, me // z_bit % nz, me % 2
    place = jnp.stack([x, y, z, core]).astype(jnp.int32)

    their_pre = across(pre_act, core_bit)

    slots = jnp.arange(dp * cap, dtype=jnp.int32)
    slots = slots - slots % (2 * cap) + slot_order(slots % (2 * cap), third)
    number = jnp.max(jnp.where(slots[:, None] == route_slot[None, :], route_row[None, :], -1), axis=1)
    number = number.reshape(dp // 2, 1, 2 * cap)
    notes = jnp.concatenate([number // 32, number % 32], axis=1).astype(BF16)
    notes = jnp.pad(notes, ((0, 0), (0, 14), (0, 128 - 2 * cap)))

    sent = gather_rows(llm_grad, route_slot, notes, dp, cap)
    sent = sent.reshape(dp, sent.shape[2], 128)
    sent, pre_act, their_pre, down_weight = lax.optimization_barrier((sent, pre_act, their_pre, down_weight))
    got = lax.all_to_all(sent, "dp", 0, 0, tiled=True)

    mine_t, slope = hidden_transposed(pre_act, True)
    (theirs_t,) = hidden_transposed(their_pre, False)
    weight_t = down_weight.T
    got, mine_t, theirs_t, slope, place, weight_t = lax.optimization_barrier(
        (got, mine_t, theirs_t, slope, place, weight_t)
    )
    mine_t = mine_t.reshape(nx, ny, nz, share, img)
    theirs_t = theirs_t.reshape(nx, ny, nz, share, img)

    notes = got[:, half // 128 * 2 * cap :][:, :2, : 2 * cap].astype(jnp.int32)
    landing = notes[:, 0] * 32 + notes[:, 1]
    landing = jnp.where(landing >= 0, landing, -1)
    lane = jnp.arange(4 * third, dtype=jnp.int32)
    landing = jnp.stack(
        [
            jnp.where(lane < cap, landing[:, : 4 * third], -1),
            jnp.where(lane >= third, landing[:, 2 * third :], -1),
        ]
    )
    grads = land_rows(place, got, landing, img, half, cap)

    others = across(grads[1], core_bit)
    firsts, seconds = {}, {}
    for shift in (1, 3, 2, 0):
        one, two = partial_pieces(mine_t, theirs_t, grads, place, shift)
        mine_t, others, _ = lax.optimization_barrier((mine_t, others, one))
        firsts[shift] = across(one, shift * x_bit) if shift else one
        seconds[shift] = across(two, shift * y_bit) if shift else two

    d_pre = d_pre_product(place, grads[0], others, weight_t, slope)
    firsts[0], seconds[0], d_pre = lax.optimization_barrier((firsts[0], seconds[0], d_pre))

    sums = first_sums(place, [firsts[k] for k in range(4)], [seconds[k] for k in range(4)], share)
    firsts = [sums[0]] + [across(sums[k], k * y_bit) for k in (1, 2, 3)]
    seconds = [sums[4]] + [across(sums[4 + k], k * x_bit) for k in (1, 2, 3)]
    total, keep, send = second_sums(place, firsts, seconds)

    total = total + over(send, z_bit, 0).astype(F32)
    for turn in range(1, n_cuts):
        total = total + over(keep, 0, turn).astype(F32) + over(send, z_bit, turn).astype(F32)

    total = (total * (1.0 / (n_cuts * dp))).reshape(2, share // 2, half)
    mine = jnp.where(core == 0, total[0], total[1])
    other = across(jnp.where(core == 0, total[1], total[0]), core_bit)
    w_grad = jnp.concatenate([jnp.where(core == 0, mine, other), jnp.where(core == 0, other, mine)], axis=1)
    return (d_pre, w_grad)


def solution(mesh):
    placed = (
        P(("cuts", "dp"), None),
        P(("cuts", "dp")),
        P(("cuts", "dp")),
        P(("cuts", "dp"), None),
        P(),
    )
    return jax.shard_map(
        functools.partial(on_device, (4, 4, 2)),
        mesh=mesh,
        in_specs=placed,
        out_specs=(P(("cuts", "dp"), None), P("dp", None)),
        check_vma=False,
    )
```

```python
import functools

import jax
import jax.numpy as jnp
from jax import lax
from jax.experimental import pallas as pl
from jax.experimental.pallas import tpu as pltpu
from jax.sharding import PartitionSpec as P

BF16 = jnp.bfloat16
VMEM = pl.BlockSpec(memory_space=pltpu.VMEM)
SMEM = pl.BlockSpec(memory_space=pltpu.SMEM)
F32 = jnp.float32
VMEM_LIMIT = 28 * 1024 * 1024
VMEM_LARGE = 54 * 1024 * 1024
VMEM_DPRE = 50 * 1024 * 1024
LANES = 512


def gelu_parts(pre_value):
    normal_cdf = 0.5 * (1.0 + lax.erf(pre_value * 0.7071067811865476))
    normal_pdf = jnp.exp(-0.5 * pre_value * pre_value) * 0.3989422804014327
    return (pre_value * normal_cdf, normal_cdf + pre_value * normal_pdf)


def dot32(a, b, contract=((1,), (0,))):
    return lax.dot_general(a, b, (contract, ((), ())), preferred_element_type=F32)


def slot_order(place, third):
    return jnp.where(
        place < 3 * third, place, jnp.where(place < 4 * third, place + 2 * third, place - third)
    )


def gather_kernel(third, route_ref, grad_ref, sent_ref, pick_ref, tile_ref, note_ref, tile_sem, note_sem):
    part = pl.program_id(0)
    last = pl.num_programs(0) - 1
    bank = lax.rem(part, 2)
    block = 6 * third
    steps, rows_per = pick_ref.shape[:2]
    chips = rows_per // block
    tiles = sent_ref.shape[2] // block

    def tile_copy(number, side):
        tile = 2 * number + side
        core = lax.div(tile, tiles)
        rows = pl.ds(pl.multiple_of(lax.rem(tile, tiles) * block, 16), block)
        return pltpu.make_async_copy(
            tile_ref.at[lax.rem(number, 2), side], sent_ref.at[:, core, rows, :], tile_sem.at[lax.rem(number, 2), side]
        )

    def note_copy(core):
        return pltpu.make_async_copy(
            note_ref, sent_ref.at[:, core, pl.ds(tiles * block, 16), :], note_sem.at[core]
        )

    @pl.when(part >= 2)
    def _():
        for side in range(2):
            tile_copy(part - 2, side).wait()

    def emit(step, pick):
        rows = dot32(pick, grad_ref[...]).astype(BF16)
        for side in range(2):
            half = rows[:, side * 128 : side * 128 + 128]
            tile_ref[bank, side, pl.ds(step * chips, chips)] = half.reshape(chips, block, 128)

    @pl.when(part == 0)
    def _():
        note_ref[...] = jnp.zeros_like(note_ref)
        line = lax.broadcasted_iota(jnp.int32, (16, block), 0)
        for step in range(steps):
            row = lax.broadcasted_iota(jnp.int32, (rows_per, 1), 0) + step * rows_per
            place = lax.rem(row, block)
            slot = row - place + slot_order(place, third)
            match = slot == route_ref[0:1, :]
            pick = jnp.where(match, 1.0, 0.0).astype(BF16)
            pick_ref[step] = pick
            emit(step, pick)
            number = jnp.sum(jnp.where(match, route_ref[1:2, :] + 1, 0).astype(F32), axis=1, keepdims=True)
            for chip in range(chips):
                wide = jnp.broadcast_to(number[chip * block : (chip + 1) * block], (block, 128))
                flat = wide.T[:16].astype(jnp.int32) - 1
                note = jnp.where(line == 0, flat >> 5, flat & 31).astype(F32).astype(BF16)
                note_ref[step * chips + chip, :, :block] = note
        for core in range(2):
            note_copy(core).start()

    @pl.when(part > 0)
    def _():
        for step in range(steps):
            emit(step, pick_ref[step])

    for side in range(2):
        tile_copy(part, side).start()

    @pl.when(part == last)
    def _():
        for side in range(2):
            tile_copy(part - 1, side).wait()
            tile_copy(part, side).wait()
            note_copy(side).wait()


def gather_rows(llm_grad, routes, dp, cap):
    rows, feat = llm_grad.shape
    half = feat // 2
    slots = dp * cap
    chips = dp // 2
    steps = 8
    return pl.pallas_call(
        functools.partial(gather_kernel, cap // 3),
        grid=(feat // 256,),
        in_specs=[
            pl.BlockSpec((2, rows), lambda n: (0, 0)),
            pl.BlockSpec((rows, 256), lambda n: (0, n)),
        ],
        out_specs=pl.BlockSpec(memory_space=pltpu.HBM),
        out_shape=pltpu.HBM((chips, 2, half // 128 * 2 * cap + 16, 128), BF16),
        scratch_shapes=[
            pltpu.VMEM((steps, slots // steps, rows), BF16),
            pltpu.VMEM((2, 2, chips, 2 * cap, 128), BF16),
            pltpu.VMEM((chips, 16, 128), BF16),
            pltpu.SemaphoreType.DMA((2, 2)),
            pltpu.SemaphoreType.DMA((2,)),
        ],
        compiler_params=pltpu.CompilerParams(vmem_limit_bytes=VMEM_LARGE),
        cost_estimate=pl.CostEstimate(
            flops=2 * slots * rows * feat, bytes_accessed=2 * (rows + slots) * feat, transcendentals=0
        ),
        name="gather_rows",
    )(routes, llm_grad)


def land_kernel(place_ref, got_ref, land_ref, mine_ref, theirs_ref, pick_ref):
    part = pl.program_id(0)
    last = pl.num_programs(0) - 1
    senders, both, _ = got_ref.shape
    block = both // 2
    span = 2 * block // 3
    img = mine_ref.shape[0]
    outs = (mine_ref, theirs_ref)

    @pl.when(part == 0)
    def _():
        row = lax.broadcasted_iota(jnp.int32, (img, 1), 0)
        for side in range(2):
            pick_ref[side] = jnp.where(row == land_ref[side ^ place_ref[3]], 1.0, 0.0).astype(BF16)

    def rows(side, tile):
        begin = pl.multiple_of((side ^ place_ref[3]) * (block - span) + tile * block, 16)
        return got_ref[:, pl.ds(begin, span), :].reshape(senders * span, 128)

    for side in range(2):

        @pl.when(part < last)
        def _(side=side):
            right = jnp.concatenate([rows(side, 0), rows(side, 1)], axis=1)
            outs[side][...] = dot32(pick_ref[side], right).astype(BF16)

        @pl.when(part == last)
        def _(side=side):
            outs[side][:, :128] = dot32(pick_ref[side], rows(side, 0)).astype(BF16)


def land_rows(place, got, landing, img, half, cap):
    dp = got.shape[0]
    span = 4 * cap // 3
    return pl.pallas_call(
        land_kernel,
        grid_spec=pltpu.PrefetchScalarGridSpec(
            num_scalar_prefetch=1,
            grid=(pl.cdiv(half, 256),),
            in_specs=[
                pl.BlockSpec((dp, 4 * cap, 128), lambda n, p: (0, n, 0)),
                pl.BlockSpec((2, 1, dp * span), lambda n, p: (0, 0, 0)),
            ],
            out_specs=[pl.BlockSpec((img, 256), lambda n, p: (0, n))] * 2,
            scratch_shapes=[pltpu.VMEM((2, img, dp * span), BF16)],
        ),
        out_shape=[jax.ShapeDtypeStruct((img, half), BF16)] * 2,
        compiler_params=pltpu.CompilerParams(vmem_limit_bytes=VMEM_LIMIT),
        cost_estimate=pl.CostEstimate(
            flops=4 * img * dp * span * half, bytes_accessed=4 * half * (dp * cap + img), transcendentals=0
        ),
        name="land_rows",
    )(place, got, landing.reshape(2, 1, dp * span))


def hidden_kernel(pre_ref, out_ref, *slope_ref):
    value, slope = gelu_parts(pre_ref[...].astype(F32))
    out_ref[...] = value.T.astype(BF16)
    if slope_ref:
        slope_ref[0][...] = slope


def hidden_transposed(pre_act, with_slope):
    img, hid = pre_act.shape
    out = [(pl.BlockSpec((256, img), lambda n: (n, 0)), jax.ShapeDtypeStruct((hid, img), BF16))]
    if with_slope:
        out.append((pl.BlockSpec((img, 256), lambda n: (0, n)), pltpu.HBM((img, hid), F32)))
    return pl.pallas_call(
        hidden_kernel,
        grid=(hid // 256,),
        in_specs=[pl.BlockSpec((img, 256), lambda n: (0, n))],
        out_specs=[spec for spec, _ in out],
        out_shape=[kind for _, kind in out],
        compiler_params=pltpu.CompilerParams(vmem_limit_bytes=VMEM_LARGE),
        cost_estimate=pl.CostEstimate(
            flops=30 * img * hid, bytes_accessed=4 * img * hid, transcendentals=img * hid
        ),
        name="hidden_transposed",
    )(pre_act)


def d_pre_kernel(place_ref, mine_ref, theirs_ref, weight_ref, slope_ref, out_ref, both_ref):
    half = mine_ref.shape[1]

    @pl.when(pl.program_id(0) == 0)
    def _():
        core = place_ref[3]
        both_ref[:, pl.ds(pl.multiple_of(core * half, 128), half)] = mine_ref[...]
        both_ref[:, pl.ds(pl.multiple_of((1 - core) * half, 128), half)] = theirs_ref[...]

    for at in range(0, LANES, 256):
        lane = slice(at, at + 256)
        total = dot32(both_ref[...], weight_ref[:, lane])
        out_ref[:, lane] = (total * slope_ref[:, lane]).astype(BF16)


def d_pre_product(place, mine, theirs, weight_t, slope):
    img, half = mine.shape
    hid = weight_t.shape[1]
    return pl.pallas_call(
        d_pre_kernel,
        grid_spec=pltpu.PrefetchScalarGridSpec(
            num_scalar_prefetch=1,
            grid=(hid // LANES,),
            in_specs=[
                VMEM,
                VMEM,
                pl.BlockSpec((2 * half, LANES), lambda n, p: (0, n)),
                pl.BlockSpec((img, LANES), lambda n, p: (0, n)),
            ],
            out_specs=pl.BlockSpec((img, LANES), lambda n, p: (0, n)),
            scratch_shapes=[pltpu.VMEM((img, 2 * half), BF16)],
        ),
        out_shape=pltpu.HBM((img, hid), BF16),
        compiler_params=pltpu.CompilerParams(vmem_limit_bytes=VMEM_DPRE),
        cost_estimate=pl.CostEstimate(
            flops=4 * img * half * hid, bytes_accessed=4 * hid * half + 6 * img * hid, transcendentals=0
        ),
        name="d_pre",
    )(place, mine, theirs, weight_t, slope)


def partial_kernel(shift, place_ref, mine_ref, theirs_ref, near_ref, far_ref, first_ref, second_ref):
    img = near_ref.shape[0]
    for stream, out in enumerate((first_ref, second_ref)):
        at = place_ref[stream] ^ shift
        total = 0.0
        for left, grad in ((mine_ref, near_ref), (theirs_ref, far_ref)):
            block = left[:, at, 1] if stream else left[at, :, 0]
            total = total + dot32(block.reshape(out.shape[0], img), grad[...])
        out[...] = total.astype(out.dtype)


def partial_pieces(mine_t, theirs_t, grads, place, shift):
    nx, ny, _, share, img = mine_t.shape
    half = grads[0].shape[1]
    return pl.pallas_call(
        functools.partial(partial_kernel, shift),
        in_specs=[SMEM] + [VMEM] * 4,
        out_specs=[VMEM] * 2,
        out_shape=[jax.ShapeDtypeStruct((n * share, half), BF16 if shift else F32) for n in (ny, nx)],
        compiler_params=pltpu.CompilerParams(vmem_limit_bytes=VMEM_LIMIT),
        cost_estimate=pl.CostEstimate(
            flops=4 * (nx + ny) * share * img * half,
            bytes_accessed=4 * img * ((nx + ny) * share + half),
            transcendentals=0,
        ),
        name=f"partial_pieces_{shift}",
    )(place, mine_t, theirs_t, *grads)


def first_sum_kernel(place_ref, *refs):
    for stream in range(2):
        own, one, two, three = refs[4 * stream : 4 * stream + 4]
        for k, out in enumerate(refs[8 + 4 * stream : 12 + 4 * stream]):
            share = out.shape[0]
            rows = pl.ds(pl.multiple_of((place_ref[1 - stream] ^ k) * share, 16), share)
            total = own[rows] + one[rows].astype(F32) + two[rows].astype(F32) + three[rows].astype(F32)
            out[...] = total.astype(out.dtype)


def first_sums(place, firsts, seconds, share):
    half = firsts[0].shape[1]
    outs = ([jax.ShapeDtypeStruct((share, half), F32)] + [jax.ShapeDtypeStruct((share, half), BF16)] * 3) * 2
    return pl.pallas_call(
        first_sum_kernel,
        in_specs=[SMEM] + [VMEM] * 8,
        out_specs=[VMEM] * 8,
        out_shape=outs,
        compiler_params=pltpu.CompilerParams(vmem_limit_bytes=VMEM_LIMIT),
        cost_estimate=pl.CostEstimate(
            flops=32 * share * half, bytes_accessed=100 * share * half, transcendentals=0
        ),
        name="first_sums",
    )(place, *firsts, *seconds)


def second_sum_kernel(place_ref, *refs):
    ones, twos = refs[:4], refs[4:8]
    own_ref, keep_ref, send_ref = refs[8:]
    first = ones[0][...] + sum(r[...].astype(F32) for r in ones[1:])
    second = twos[0][...] + sum(r[...].astype(F32) for r in twos[1:])
    low = place_ref[2] == 0
    own = jnp.where(low, first, second)
    own_ref[...] = own
    keep_ref[...] = own.astype(BF16)
    send_ref[...] = jnp.where(low, second, first).astype(BF16)


def second_sums(place, firsts, seconds):
    share, half = firsts[0].shape
    vmem = pl.BlockSpec(memory_space=pltpu.VMEM)
    return pl.pallas_call(
        second_sum_kernel,
        in_specs=[pl.BlockSpec(memory_space=pltpu.SMEM)] + [vmem] * 8,
        out_specs=[vmem] * 3,
        out_shape=[jax.ShapeDtypeStruct((share, half), kind) for kind in (F32, BF16, BF16)],
        compiler_params=pltpu.CompilerParams(vmem_limit_bytes=VMEM_LIMIT),
        cost_estimate=pl.CostEstimate(
            flops=8 * share * half, bytes_accessed=28 * share * half, transcendentals=0
        ),
        name="second_sums",
    )(place, *firsts, *seconds)


def on_device(shape, llm_grad, route_slot, route_row, pre_act, down_weight):
    nx, ny, nz = shape
    dp = lax.axis_size("dp")
    n_cuts = lax.axis_size("cuts")
    img, hid = pre_act.shape
    half = llm_grad.shape[1] // 2
    cap = 2 * img // dp
    third = cap // 3
    share = 2 * hid // dp
    core_bit, z_bit, y_bit, x_bit = 1, 2, 2 * nz, 2 * nz * ny

    def across(value, mask):
        return lax.ppermute(value, "dp", [(i, i ^ mask) for i in range(dp)])

    def over(value, mask, turn):
        pairs = [
            (c * dp + i, ((c + turn) % n_cuts) * dp + (i ^ mask)) for c in range(n_cuts) for i in range(dp)
        ]
        return lax.ppermute(value, ("cuts", "dp"), pairs)

    me = lax.axis_index("dp").astype(jnp.int32)
    x, y, z, core = me // x_bit, me // y_bit % ny, me // z_bit % nz, me % 2
    place = jnp.stack([x, y, z, core]).astype(jnp.int32)

    their_pre = across(pre_act, core_bit)

    sent = gather_rows(llm_grad, jnp.stack([route_slot, route_row]), dp, cap)
    sent = sent.reshape(dp, sent.shape[2], 128)
    sent, pre_act, their_pre, down_weight = lax.optimization_barrier((sent, pre_act, their_pre, down_weight))
    got = lax.all_to_all(sent, "dp", 0, 0, tiled=True)

    mine_t, slope = hidden_transposed(pre_act, True)
    (theirs_t,) = hidden_transposed(their_pre, False)
    weight_t = down_weight.T
    got, mine_t, theirs_t, slope, place, weight_t = lax.optimization_barrier(
        (got, mine_t, theirs_t, slope, place, weight_t)
    )
    mine_t = mine_t.reshape(nx, ny, nz, share, img)
    theirs_t = theirs_t.reshape(nx, ny, nz, share, img)

    notes = got[:, half // 128 * 2 * cap :][:, :2, : 2 * cap].astype(jnp.int32)
    landing = notes[:, 0] * 32 + notes[:, 1]
    landing = jnp.where(landing >= 0, landing, -1)
    lane = jnp.arange(4 * third, dtype=jnp.int32)
    landing = jnp.stack(
        [
            jnp.where(lane < cap, landing[:, : 4 * third], -1),
            jnp.where(lane >= third, landing[:, 2 * third :], -1),
        ]
    )
    grads = land_rows(place, got, landing, img, half, cap)

    others = across(grads[1], core_bit)
    firsts, seconds = {}, {}
    for shift in (1, 3, 2, 0):
        one, two = partial_pieces(mine_t, theirs_t, grads, place, shift)
        mine_t, others, _ = lax.optimization_barrier((mine_t, others, one))
        firsts[shift] = across(one, shift * x_bit) if shift else one
        seconds[shift] = across(two, shift * y_bit) if shift else two

    d_pre = d_pre_product(place, grads[0], others, weight_t, slope)
    firsts[0], seconds[0], d_pre = lax.optimization_barrier((firsts[0], seconds[0], d_pre))

    sums = first_sums(place, [firsts[k] for k in range(4)], [seconds[k] for k in range(4)], share)
    firsts = [sums[0]] + [across(sums[k], k * y_bit) for k in (1, 2, 3)]
    seconds = [sums[4]] + [across(sums[4 + k], k * x_bit) for k in (1, 2, 3)]
    total, keep, send = second_sums(place, firsts, seconds)

    total = total + over(send, z_bit, 0).astype(F32)
    for turn in range(1, n_cuts):
        total = total + over(keep, 0, turn).astype(F32) + over(send, z_bit, turn).astype(F32)

    total = (total * (1.0 / (n_cuts * dp))).reshape(2, share // 2, half)
    mine = jnp.where(core == 0, total[0], total[1])
    other = across(jnp.where(core == 0, total[1], total[0]), core_bit)
    w_grad = jnp.concatenate([jnp.where(core == 0, mine, other), jnp.where(core == 0, other, mine)], axis=1)
    return (d_pre, w_grad)


def solution(mesh):
    placed = (
        P(("cuts", "dp"), None),
        P(("cuts", "dp")),
        P(("cuts", "dp")),
        P(("cuts", "dp"), None),
        P(),
    )
    return jax.shard_map(
        functools.partial(on_device, (4, 4, 2)),
        mesh=mesh,
        in_specs=placed,
        out_specs=(P(("cuts", "dp"), None), P("dp", None)),
        check_vma=False,
    )
```

```python
import functools

import jax
import jax.numpy as jnp
from jax import lax
from jax.experimental import pallas as pl
from jax.experimental.pallas import tpu as pltpu
from jax.sharding import PartitionSpec as P

BF16 = jnp.bfloat16
VMEM = pl.BlockSpec(memory_space=pltpu.VMEM)
SMEM = pl.BlockSpec(memory_space=pltpu.SMEM)
F32 = jnp.float32
VMEM_LIMIT = 28 * 1024 * 1024
VMEM_LARGE = 54 * 1024 * 1024
VMEM_DPRE = 50 * 1024 * 1024
LANES = 512


def gelu_parts(pre_value):
    normal_cdf = 0.5 * (1.0 + lax.erf(pre_value * 0.7071067811865476))
    normal_pdf = jnp.exp(-0.5 * pre_value * pre_value) * 0.3989422804014327
    return (pre_value * normal_cdf, normal_cdf + pre_value * normal_pdf)


def dot32(a, b, contract=((1,), (0,))):
    return lax.dot_general(a, b, (contract, ((), ())), preferred_element_type=F32)


def slot_order(place, third):
    return jnp.where(
        place < 3 * third, place, jnp.where(place < 4 * third, place + 2 * third, place - third)
    )


def gather_kernel(third, slot_ref, row_ref, grad_ref, sent_ref, pick_ref, tile_ref, note_ref, tile_sem, note_sem):
    part = pl.program_id(0)
    last = pl.num_programs(0) - 1
    bank = lax.rem(part, 2)
    block = 6 * third
    steps, rows_per = pick_ref.shape[:2]
    chips = rows_per // block
    tiles = sent_ref.shape[2] // block

    def tile_copy(number, side):
        tile = 2 * number + side
        core = lax.div(tile, tiles)
        rows = pl.ds(pl.multiple_of(lax.rem(tile, tiles) * block, 16), block)
        return pltpu.make_async_copy(
            tile_ref.at[lax.rem(number, 2), side], sent_ref.at[:, core, rows, :], tile_sem.at[lax.rem(number, 2), side]
        )

    def note_copy(core):
        return pltpu.make_async_copy(
            note_ref, sent_ref.at[:, core, pl.ds(tiles * block, 16), :], note_sem.at[core]
        )

    @pl.when(part >= 2)
    def _():
        for side in range(2):
            tile_copy(part - 2, side).wait()

    def emit(step, pick):
        rows = dot32(pick, grad_ref[...]).astype(BF16)
        for side in range(2):
            half = rows[:, side * 128 : side * 128 + 128]
            tile_ref[bank, side, pl.ds(step * chips, chips)] = half.reshape(chips, block, 128)

    @pl.when(part == 0)
    def _():
        note_ref[...] = jnp.zeros_like(note_ref)
        line = lax.broadcasted_iota(jnp.int32, (16, block), 0)
        slots, numbers = (
            jnp.concatenate([ref[at : at + 1, :] for at in range(ref.shape[0])], axis=1)
            for ref in (slot_ref, row_ref)
        )
        for step in range(steps):
            row = lax.broadcasted_iota(jnp.int32, (rows_per, 1), 0) + step * rows_per
            place = lax.rem(row, block)
            slot = row - place + slot_order(place, third)
            match = slot == slots
            pick = jnp.where(match, 1.0, 0.0).astype(BF16)
            pick_ref[step] = pick
            emit(step, pick)
            number = jnp.sum(jnp.where(match, numbers + 1, 0).astype(F32), axis=1, keepdims=True)
            for chip in range(chips):
                wide = jnp.broadcast_to(number[chip * block : (chip + 1) * block], (block, 128))
                flat = wide.T[:16].astype(jnp.int32) - 1
                note = jnp.where(line == 0, flat >> 5, flat & 31).astype(F32).astype(BF16)
                note_ref[step * chips + chip, :, :block] = note
        for core in range(2):
            note_copy(core).start()

    @pl.when(part > 0)
    def _():
        for step in range(steps):
            emit(step, pick_ref[step])

    for side in range(2):
        tile_copy(part, side).start()

    @pl.when(part == last)
    def _():
        for side in range(2):
            tile_copy(part - 1, side).wait()
            tile_copy(part, side).wait()
            note_copy(side).wait()


def gather_rows(llm_grad, route_slot, route_row, dp, cap):
    rows, feat = llm_grad.shape
    half = feat // 2
    slots = dp * cap
    chips = dp // 2
    steps = 8
    return pl.pallas_call(
        functools.partial(gather_kernel, cap // 3),
        grid=(feat // 256,),
        in_specs=[
            pl.BlockSpec((rows // 128, 128), lambda n: (0, 0)),
            pl.BlockSpec((rows // 128, 128), lambda n: (0, 0)),
            pl.BlockSpec((rows, 256), lambda n: (0, n)),
        ],
        out_specs=pl.BlockSpec(memory_space=pltpu.HBM),
        out_shape=pltpu.HBM((chips, 2, half // 128 * 2 * cap + 16, 128), BF16),
        scratch_shapes=[
            pltpu.VMEM((steps, slots // steps, rows), BF16),
            pltpu.VMEM((2, 2, chips, 2 * cap, 128), BF16),
            pltpu.VMEM((chips, 16, 128), BF16),
            pltpu.SemaphoreType.DMA((2, 2)),
            pltpu.SemaphoreType.DMA((2,)),
        ],
        compiler_params=pltpu.CompilerParams(vmem_limit_bytes=VMEM_LARGE),
        cost_estimate=pl.CostEstimate(
            flops=2 * slots * rows * feat, bytes_accessed=2 * (rows + slots) * feat, transcendentals=0
        ),
        name="gather_rows",
    )(route_slot.reshape(rows // 128, 128), route_row.reshape(rows // 128, 128), llm_grad)


def land_kernel(place_ref, got_ref, land_ref, mine_ref, theirs_ref, pick_ref):
    part = pl.program_id(0)
    last = pl.num_programs(0) - 1
    senders, block, _ = got_ref.shape
    block = block // 2
    span = 2 * block // 3
    img = mine_ref.shape[0]
    outs = (mine_ref, theirs_ref)

    def rows(side, tile):
        begin = pl.multiple_of((side ^ place_ref[3]) * (block - span) + tile * block, 16)
        return got_ref[:, pl.ds(begin, span), :].reshape(senders * span, 128)

    def both(side):
        return jnp.concatenate([rows(side, 0), rows(side, 1)], axis=1)

    @pl.when(part == 0)
    def _():
        count = img // 4
        for side in range(2):
            right = both(side)
            land = land_ref[side ^ place_ref[3]]
            for begin in range(0, img, count):
                row = lax.broadcasted_iota(jnp.int32, (count, 1), 0) + begin
                pick = jnp.where(row == land, 1.0, 0.0).astype(BF16)
                pick_ref[side, begin : begin + count] = pick
                outs[side][begin : begin + count] = dot32(pick, right).astype(BF16)

    @pl.when((part > 0) & (part < last))
    def _():
        for side in range(2):
            outs[side][...] = dot32(pick_ref[side], both(side)).astype(BF16)

    @pl.when(part == last)
    def _():
        for side in range(2):
            outs[side][:, :128] = dot32(pick_ref[side], rows(side, 0)).astype(BF16)


def land_rows(place, got, landing, img, half, cap):
    dp = got.shape[0]
    span = 4 * cap // 3
    return pl.pallas_call(
        land_kernel,
        grid_spec=pltpu.PrefetchScalarGridSpec(
            num_scalar_prefetch=1,
            grid=(pl.cdiv(half, 256),),
            in_specs=[
                pl.BlockSpec((dp, 4 * cap, 128), lambda n, p: (0, n, 0)),
                pl.BlockSpec((2, 1, dp * span), lambda n, p: (0, 0, 0)),
            ],
            out_specs=[pl.BlockSpec((img, 256), lambda n, p: (0, n))] * 2,
            scratch_shapes=[pltpu.VMEM((2, img, dp * span), BF16)],
        ),
        out_shape=[jax.ShapeDtypeStruct((img, half), BF16)] * 2,
        compiler_params=pltpu.CompilerParams(vmem_limit_bytes=VMEM_LIMIT),
        cost_estimate=pl.CostEstimate(
            flops=4 * img * dp * span * half, bytes_accessed=4 * half * (dp * cap + img), transcendentals=0
        ),
        name="land_rows",
    )(place, got, landing.reshape(2, 1, dp * span))


def hidden_kernel(pre_ref, out_ref, *slope_ref):
    value, slope = gelu_parts(pre_ref[...].astype(F32))
    out_ref[...] = value.T.astype(BF16)
    if slope_ref:
        slope_ref[0][...] = slope


def hidden_transposed(pre_act, with_slope):
    img, hid = pre_act.shape
    out = [(pl.BlockSpec((256, img), lambda n: (n, 0)), jax.ShapeDtypeStruct((hid, img), BF16))]
    if with_slope:
        out.append((pl.BlockSpec((img, 256), lambda n: (0, n)), pltpu.HBM((img, hid), F32)))
    return pl.pallas_call(
        hidden_kernel,
        grid=(hid // 256,),
        in_specs=[pl.BlockSpec((img, 256), lambda n: (0, n))],
        out_specs=[spec for spec, _ in out],
        out_shape=[kind for _, kind in out],
        compiler_params=pltpu.CompilerParams(vmem_limit_bytes=VMEM_LARGE),
        cost_estimate=pl.CostEstimate(
            flops=30 * img * hid, bytes_accessed=4 * img * hid, transcendentals=img * hid
        ),
        name="hidden_transposed",
    )(pre_act)


def d_pre_kernel(place_ref, mine_ref, theirs_ref, weight_ref, slope_ref, out_ref, both_ref):
    half = mine_ref.shape[1]

    @pl.when(pl.program_id(0) == 0)
    def _():
        core = place_ref[3]
        both_ref[:, pl.ds(pl.multiple_of(core * half, 128), half)] = mine_ref[...]
        both_ref[:, pl.ds(pl.multiple_of((1 - core) * half, 128), half)] = theirs_ref[...]

    for at in range(0, LANES, 256):
        lane = slice(at, at + 256)
        total = dot32(both_ref[...], weight_ref[:, lane])
        out_ref[:, lane] = (total * slope_ref[:, lane]).astype(BF16)


def d_pre_product(place, mine, theirs, weight_t, slope):
    img, half = mine.shape
    hid = weight_t.shape[1]
    return pl.pallas_call(
        d_pre_kernel,
        grid_spec=pltpu.PrefetchScalarGridSpec(
            num_scalar_prefetch=1,
            grid=(hid // LANES,),
            in_specs=[
                VMEM,
                VMEM,
                pl.BlockSpec((2 * half, LANES), lambda n, p: (0, n)),
                pl.BlockSpec((img, LANES), lambda n, p: (0, n)),
            ],
            out_specs=pl.BlockSpec((img, LANES), lambda n, p: (0, n)),
            scratch_shapes=[pltpu.VMEM((img, 2 * half), BF16)],
        ),
        out_shape=pltpu.HBM((img, hid), BF16),
        compiler_params=pltpu.CompilerParams(vmem_limit_bytes=VMEM_DPRE),
        cost_estimate=pl.CostEstimate(
            flops=4 * img * half * hid, bytes_accessed=4 * hid * half + 6 * img * hid, transcendentals=0
        ),
        name="d_pre",
    )(place, mine, theirs, weight_t, slope)


def partial_kernel(shift, place_ref, mine_ref, theirs_ref, near_ref, far_ref, first_ref, second_ref):
    img = near_ref.shape[0]
    for stream, out in enumerate((first_ref, second_ref)):
        at = place_ref[stream] ^ shift
        total = 0.0
        for left, grad in ((mine_ref, near_ref), (theirs_ref, far_ref)):
            block = left[:, at, 1] if stream else left[at, :, 0]
            total = total + dot32(block.reshape(out.shape[0], img), grad[...])
        out[...] = total.astype(out.dtype)


def partial_pieces(mine_t, theirs_t, grads, place, shift):
    nx, ny, _, share, img = mine_t.shape
    half = grads[0].shape[1]
    return pl.pallas_call(
        functools.partial(partial_kernel, shift),
        in_specs=[SMEM] + [VMEM] * 4,
        out_specs=[VMEM] * 2,
        out_shape=[jax.ShapeDtypeStruct((n * share, half), BF16 if shift else F32) for n in (ny, nx)],
        compiler_params=pltpu.CompilerParams(vmem_limit_bytes=VMEM_LIMIT),
        cost_estimate=pl.CostEstimate(
            flops=4 * (nx + ny) * share * img * half,
            bytes_accessed=4 * img * ((nx + ny) * share + half),
            transcendentals=0,
        ),
        name=f"partial_pieces_{shift}",
    )(place, mine_t, theirs_t, *grads)


def first_sum_kernel(place_ref, *refs):
    for stream in range(2):
        own, one, two, three = refs[4 * stream : 4 * stream + 4]
        for k, out in enumerate(refs[8 + 4 * stream : 12 + 4 * stream]):
            share = out.shape[0]
            rows = pl.ds(pl.multiple_of((place_ref[1 - stream] ^ k) * share, 16), share)
            total = own[rows] + one[rows].astype(F32) + two[rows].astype(F32) + three[rows].astype(F32)
            out[...] = total.astype(out.dtype)


def first_sums(place, firsts, seconds, share):
    half = firsts[0].shape[1]
    outs = ([jax.ShapeDtypeStruct((share, half), F32)] + [jax.ShapeDtypeStruct((share, half), BF16)] * 3) * 2
    return pl.pallas_call(
        first_sum_kernel,
        in_specs=[SMEM] + [VMEM] * 8,
        out_specs=[VMEM] * 8,
        out_shape=outs,
        compiler_params=pltpu.CompilerParams(vmem_limit_bytes=VMEM_LIMIT),
        cost_estimate=pl.CostEstimate(
            flops=32 * share * half, bytes_accessed=100 * share * half, transcendentals=0
        ),
        name="first_sums",
    )(place, *firsts, *seconds)


def second_sum_kernel(place_ref, *refs):
    ones, twos = refs[:4], refs[4:8]
    own_ref, keep_ref, send_ref = refs[8:]
    first = ones[0][...] + sum(r[...].astype(F32) for r in ones[1:])
    second = twos[0][...] + sum(r[...].astype(F32) for r in twos[1:])
    low = place_ref[2] == 0
    own = jnp.where(low, first, second)
    own_ref[...] = own
    keep_ref[...] = own.astype(BF16)
    send_ref[...] = jnp.where(low, second, first).astype(BF16)


def second_sums(place, firsts, seconds):
    share, half = firsts[0].shape
    vmem = pl.BlockSpec(memory_space=pltpu.VMEM)
    return pl.pallas_call(
        second_sum_kernel,
        in_specs=[pl.BlockSpec(memory_space=pltpu.SMEM)] + [vmem] * 8,
        out_specs=[vmem] * 3,
        out_shape=[jax.ShapeDtypeStruct((share, half), kind) for kind in (F32, BF16, BF16)],
        compiler_params=pltpu.CompilerParams(vmem_limit_bytes=VMEM_LIMIT),
        cost_estimate=pl.CostEstimate(
            flops=8 * share * half, bytes_accessed=28 * share * half, transcendentals=0
        ),
        name="second_sums",
    )(place, *firsts, *seconds)


def on_device(shape, llm_grad, route_slot, route_row, pre_act, down_weight):
    nx, ny, nz = shape
    dp = lax.axis_size("dp")
    n_cuts = lax.axis_size("cuts")
    img, hid = pre_act.shape
    half = llm_grad.shape[1] // 2
    cap = 2 * img // dp
    third = cap // 3
    share = 2 * hid // dp
    core_bit, z_bit, y_bit, x_bit = 1, 2, 2 * nz, 2 * nz * ny

    def across(value, mask):
        return lax.ppermute(value, "dp", [(i, i ^ mask) for i in range(dp)])

    def over(value, mask, turn):
        pairs = [
            (c * dp + i, ((c + turn) % n_cuts) * dp + (i ^ mask)) for c in range(n_cuts) for i in range(dp)
        ]
        return lax.ppermute(value, ("cuts", "dp"), pairs)

    me = lax.axis_index("dp").astype(jnp.int32)
    x, y, z, core = me // x_bit, me // y_bit % ny, me // z_bit % nz, me % 2
    place = jnp.stack([x, y, z, core]).astype(jnp.int32)

    their_pre = across(pre_act, core_bit)

    sent = gather_rows(llm_grad, route_slot, route_row, dp, cap)
    sent = sent.reshape(dp, sent.shape[2], 128)
    sent, pre_act, their_pre, down_weight = lax.optimization_barrier((sent, pre_act, their_pre, down_weight))
    got = lax.all_to_all(sent, "dp", 0, 0, tiled=True)

    mine_t, slope = hidden_transposed(pre_act, True)
    (theirs_t,) = hidden_transposed(their_pre, False)
    weight_t = down_weight.T
    got, mine_t, theirs_t, slope, place, weight_t = lax.optimization_barrier(
        (got, mine_t, theirs_t, slope, place, weight_t)
    )
    mine_t = mine_t.reshape(nx, ny, nz, share, img)
    theirs_t = theirs_t.reshape(nx, ny, nz, share, img)

    notes = got[:, half // 128 * 2 * cap :][:, :2, : 2 * cap].astype(jnp.int32)
    landing = notes[:, 0] * 32 + notes[:, 1]
    landing = jnp.where(landing >= 0, landing, -1)
    lane = jnp.arange(4 * third, dtype=jnp.int32)
    landing = jnp.stack(
        [
            jnp.where(lane < cap, landing[:, : 4 * third], -1),
            jnp.where(lane >= third, landing[:, 2 * third :], -1),
        ]
    )
    grads = land_rows(place, got, landing, img, half, cap)

    others = across(grads[1], core_bit)
    firsts, seconds = {}, {}
    for shifts in ((1, 3), (2,), (0,)):
        made = {shift: partial_pieces(mine_t, theirs_t, grads, place, shift) for shift in shifts}
        mine_t, others, made = lax.optimization_barrier((mine_t, others, made))
        for shift, (one, two) in made.items():
            firsts[shift] = across(one, shift * x_bit) if shift else one
            seconds[shift] = across(two, shift * y_bit) if shift else two

    d_pre = d_pre_product(place, grads[0], others, weight_t, slope)
    firsts[0], seconds[0], d_pre = lax.optimization_barrier((firsts[0], seconds[0], d_pre))

    sums = first_sums(place, [firsts[k] for k in range(4)], [seconds[k] for k in range(4)], share)
    firsts = [sums[0]] + [across(sums[k], k * y_bit) for k in (1, 2, 3)]
    seconds = [sums[4]] + [across(sums[4 + k], k * x_bit) for k in (1, 2, 3)]
    total, keep, send = second_sums(place, firsts, seconds)

    total = total + over(send, z_bit, 0).astype(F32)
    for turn in range(1, n_cuts):
        total = total + over(keep, 0, turn).astype(F32) + over(send, z_bit, turn).astype(F32)

    total = (total * (1.0 / (n_cuts * dp))).reshape(2, share // 2, half)
    mine = jnp.where(core == 0, total[0], total[1])
    other = across(jnp.where(core == 0, total[1], total[0]), core_bit)
    w_grad = jnp.concatenate([jnp.where(core == 0, mine, other), jnp.where(core == 0, other, mine)], axis=1)
    return (d_pre, w_grad)


def solution(mesh):
    placed = (
        P(("cuts", "dp"), None),
        P(("cuts", "dp")),
        P(("cuts", "dp")),
        P(("cuts", "dp"), None),
        P(),
    )
    return jax.shard_map(
        functools.partial(on_device, (4, 4, 2)),
        mesh=mesh,
        in_specs=placed,
        out_specs=(P(("cuts", "dp"), None), P("dp", None)),
        check_vma=False,
    )
```

```python
import functools

import jax
import jax.numpy as jnp
from jax import lax
from jax.experimental import pallas as pl
from jax.experimental.pallas import tpu as pltpu
from jax.sharding import PartitionSpec as P

BF16 = jnp.bfloat16
VMEM = pl.BlockSpec(memory_space=pltpu.VMEM)
SMEM = pl.BlockSpec(memory_space=pltpu.SMEM)
F32 = jnp.float32
VMEM_LIMIT = 28 * 1024 * 1024
VMEM_LARGE = 54 * 1024 * 1024
VMEM_DPRE = 50 * 1024 * 1024
LANES = 512


def gelu_parts(pre_value):
    normal_cdf = 0.5 * (1.0 + lax.erf(pre_value * 0.7071067811865476))
    normal_pdf = jnp.exp(-0.5 * pre_value * pre_value) * 0.3989422804014327
    return (pre_value * normal_cdf, normal_cdf + pre_value * normal_pdf)


def dot32(a, b, contract=((1,), (0,))):
    return lax.dot_general(a, b, (contract, ((), ())), preferred_element_type=F32)


def slot_order(place, third):
    return jnp.where(
        place < 3 * third, place, jnp.where(place < 4 * third, place + 2 * third, place - third)
    )


def gather_kernel(third, slot_ref, row_ref, grad_ref, sent_ref, pick_ref, tile_ref, note_ref, tile_sem, note_sem):
    part = pl.program_id(0)
    last = pl.num_programs(0) - 1
    bank = lax.rem(part, 2)
    block = 6 * third
    steps, rows_per = pick_ref.shape[:2]
    chips = rows_per // block
    tiles = sent_ref.shape[2] // block

    def tile_copy(number, side):
        tile = 2 * number + side
        core = lax.div(tile, tiles)
        rows = pl.ds(pl.multiple_of(lax.rem(tile, tiles) * block, 16), block)
        return pltpu.make_async_copy(
            tile_ref.at[lax.rem(number, 2), side], sent_ref.at[:, core, rows, :], tile_sem.at[lax.rem(number, 2), side]
        )

    def note_copy(core):
        return pltpu.make_async_copy(
            note_ref, sent_ref.at[:, core, pl.ds(tiles * block, 16), :], note_sem.at[core]
        )

    @pl.when(part >= 2)
    def _():
        for side in range(2):
            tile_copy(part - 2, side).wait()

    def emit(step, pick):
        rows = dot32(pick, grad_ref[...]).astype(BF16)
        for side in range(2):
            half = rows[:, side * 128 : side * 128 + 128]
            tile_ref[bank, side, pl.ds(step * chips, chips)] = half.reshape(chips, block, 128)

    @pl.when(part == 0)
    def _():
        note_ref[...] = jnp.zeros_like(note_ref)
        line = lax.broadcasted_iota(jnp.int32, (16, block), 0)
        slots, numbers = (
            jnp.concatenate([ref[at : at + 1, :] for at in range(ref.shape[0])], axis=1)
            for ref in (slot_ref, row_ref)
        )
        for step in range(steps):
            row = lax.broadcasted_iota(jnp.int32, (rows_per, 1), 0) + step * rows_per
            place = lax.rem(row, block)
            slot = row - place + slot_order(place, third)
            match = slot == slots
            pick = jnp.where(match, 1.0, 0.0).astype(BF16)
            pick_ref[step] = pick
            emit(step, pick)
            number = jnp.sum(jnp.where(match, numbers + 1, 0).astype(F32), axis=1, keepdims=True)
            for chip in range(chips):
                wide = jnp.broadcast_to(number[chip * block : (chip + 1) * block], (block, 128))
                flat = wide.T[:16].astype(jnp.int32) - 1
                note = jnp.where(line == 0, flat >> 5, flat & 31).astype(F32).astype(BF16)
                note_ref[step * chips + chip, :, :block] = note
        for core in range(2):
            note_copy(core).start()

    @pl.when(part > 0)
    def _():
        for step in range(steps):
            emit(step, pick_ref[step])

    for side in range(2):
        tile_copy(part, side).start()

    @pl.when(part == last)
    def _():
        for side in range(2):
            tile_copy(part - 1, side).wait()
            tile_copy(part, side).wait()
            note_copy(side).wait()


def gather_rows(llm_grad, route_slot, route_row, dp, cap):
    rows, feat = llm_grad.shape
    half = feat // 2
    slots = dp * cap
    chips = dp // 2
    steps = 8
    return pl.pallas_call(
        functools.partial(gather_kernel, cap // 3),
        grid=(feat // 256,),
        in_specs=[
            pl.BlockSpec((rows // 128, 128), lambda n: (0, 0)),
            pl.BlockSpec((rows // 128, 128), lambda n: (0, 0)),
            pl.BlockSpec((rows, 256), lambda n: (0, n)),
        ],
        out_specs=pl.BlockSpec(memory_space=pltpu.HBM),
        out_shape=pltpu.HBM((chips, 2, half // 128 * 2 * cap + 16, 128), BF16),
        scratch_shapes=[
            pltpu.VMEM((steps, slots // steps, rows), BF16),
            pltpu.VMEM((2, 2, chips, 2 * cap, 128), BF16),
            pltpu.VMEM((chips, 16, 128), BF16),
            pltpu.SemaphoreType.DMA((2, 2)),
            pltpu.SemaphoreType.DMA((2,)),
        ],
        compiler_params=pltpu.CompilerParams(vmem_limit_bytes=VMEM_LARGE),
        cost_estimate=pl.CostEstimate(
            flops=2 * slots * rows * feat, bytes_accessed=2 * (rows + slots) * feat, transcendentals=0
        ),
        name="gather_rows",
    )(route_slot.reshape(rows // 128, 128), route_row.reshape(rows // 128, 128), llm_grad)


def land_kernel(place_ref, got_ref, land_ref, mine_ref, theirs_ref, pick_ref):
    part = pl.program_id(0)
    last = pl.num_programs(0) - 1
    senders, block, _ = got_ref.shape
    block = block // 2
    span = 2 * block // 3
    img = mine_ref.shape[0]
    outs = (mine_ref, theirs_ref)

    def rows(side, tile):
        begin = pl.multiple_of((side ^ place_ref[3]) * (block - span) + tile * block, 16)
        return got_ref[:, pl.ds(begin, span), :].reshape(senders * span, 128)

    def both(side):
        return jnp.concatenate([rows(side, 0), rows(side, 1)], axis=1)

    @pl.when(part == 0)
    def _():
        count = img // 4
        for side in range(2):
            right = both(side)
            land = land_ref[side ^ place_ref[3]]
            for begin in range(0, img, count):
                row = lax.broadcasted_iota(jnp.int32, (count, 1), 0) + begin
                pick = jnp.where(row == land, 1.0, 0.0).astype(BF16)
                pick_ref[side, begin : begin + count] = pick
                outs[side][begin : begin + count] = dot32(pick, right).astype(BF16)

    @pl.when((part > 0) & (part < last))
    def _():
        for side in range(2):
            outs[side][...] = dot32(pick_ref[side], both(side)).astype(BF16)

    @pl.when(part == last)
    def _():
        for side in range(2):
            outs[side][:, :128] = dot32(pick_ref[side], rows(side, 0)).astype(BF16)


def land_rows(place, got, landing, img, half, cap):
    dp = got.shape[0]
    span = 4 * cap // 3
    return pl.pallas_call(
        land_kernel,
        grid_spec=pltpu.PrefetchScalarGridSpec(
            num_scalar_prefetch=1,
            grid=(pl.cdiv(half, 256),),
            in_specs=[
                pl.BlockSpec((dp, 4 * cap, 128), lambda n, p: (0, n, 0)),
                pl.BlockSpec((2, 1, dp * span), lambda n, p: (0, 0, 0)),
            ],
            out_specs=[pl.BlockSpec((img, 256), lambda n, p: (0, n))] * 2,
            scratch_shapes=[pltpu.VMEM((2, img, dp * span), BF16)],
        ),
        out_shape=[jax.ShapeDtypeStruct((img, half), BF16)] * 2,
        compiler_params=pltpu.CompilerParams(vmem_limit_bytes=VMEM_LIMIT),
        cost_estimate=pl.CostEstimate(
            flops=4 * img * dp * span * half, bytes_accessed=4 * half * (dp * cap + img), transcendentals=0
        ),
        name="land_rows",
    )(place, got, landing.reshape(2, 1, dp * span))


def hidden_kernel(pre_ref, out_ref, *slope_ref):
    value, slope = gelu_parts(pre_ref[...].astype(F32))
    out_ref[...] = value.T.astype(BF16)
    if slope_ref:
        slope_ref[0][...] = slope


def hidden_transposed(pre_act, with_slope):
    img, hid = pre_act.shape
    out = [(pl.BlockSpec((256, img), lambda n: (n, 0)), jax.ShapeDtypeStruct((hid, img), BF16))]
    if with_slope:
        out.append((pl.BlockSpec((img, 256), lambda n: (0, n)), pltpu.HBM((img, hid), F32)))
    return pl.pallas_call(
        hidden_kernel,
        grid=(hid // 256,),
        in_specs=[pl.BlockSpec((img, 256), lambda n: (0, n))],
        out_specs=[spec for spec, _ in out],
        out_shape=[kind for _, kind in out],
        compiler_params=pltpu.CompilerParams(vmem_limit_bytes=VMEM_LARGE),
        cost_estimate=pl.CostEstimate(
            flops=30 * img * hid, bytes_accessed=4 * img * hid, transcendentals=img * hid
        ),
        name="hidden_transposed",
    )(pre_act)


def d_pre_kernel(place_ref, mine_ref, theirs_ref, weight_ref, slope_ref, out_ref, both_ref):
    half = mine_ref.shape[1]

    @pl.when(pl.program_id(0) == 0)
    def _():
        core = place_ref[3]
        both_ref[:, pl.ds(pl.multiple_of(core * half, 128), half)] = mine_ref[...]
        both_ref[:, pl.ds(pl.multiple_of((1 - core) * half, 128), half)] = theirs_ref[...]

    count = both_ref.shape[0] // 4
    for begin in range(0, 4 * count, count):
        rows = slice(begin, begin + count)
        total = dot32(both_ref[rows], weight_ref[...])
        out_ref[rows] = (total * slope_ref[rows]).astype(BF16)


def d_pre_product(place, mine, theirs, weight_t, slope):
    img, half = mine.shape
    hid = weight_t.shape[1]
    return pl.pallas_call(
        d_pre_kernel,
        grid_spec=pltpu.PrefetchScalarGridSpec(
            num_scalar_prefetch=1,
            grid=(hid // LANES,),
            in_specs=[
                VMEM,
                VMEM,
                pl.BlockSpec((2 * half, LANES), lambda n, p: (0, n)),
                pl.BlockSpec((img, LANES), lambda n, p: (0, n)),
            ],
            out_specs=pl.BlockSpec((img, LANES), lambda n, p: (0, n)),
            scratch_shapes=[pltpu.VMEM((img, 2 * half), BF16)],
        ),
        out_shape=pltpu.HBM((img, hid), BF16),
        compiler_params=pltpu.CompilerParams(vmem_limit_bytes=VMEM_DPRE),
        cost_estimate=pl.CostEstimate(
            flops=4 * img * half * hid, bytes_accessed=4 * hid * half + 6 * img * hid, transcendentals=0
        ),
        name="d_pre",
    )(place, mine, theirs, weight_t, slope)


def partial_kernel(shift, place_ref, mine_ref, theirs_ref, near_ref, far_ref, first_ref, second_ref):
    img = near_ref.shape[0]
    for stream, out in enumerate((first_ref, second_ref)):
        at = place_ref[stream] ^ shift
        total = 0.0
        for left, grad in ((mine_ref, near_ref), (theirs_ref, far_ref)):
            block = left[:, at, 1] if stream else left[at, :, 0]
            total = total + dot32(block.reshape(out.shape[0], img), grad[...])
        out[...] = total.astype(out.dtype)


def partial_pieces(mine_t, theirs_t, grads, place, shift):
    nx, ny, _, share, img = mine_t.shape
    half = grads[0].shape[1]
    return pl.pallas_call(
        functools.partial(partial_kernel, shift),
        in_specs=[SMEM] + [VMEM] * 4,
        out_specs=[VMEM] * 2,
        out_shape=[jax.ShapeDtypeStruct((n * share, half), BF16 if shift else F32) for n in (ny, nx)],
        compiler_params=pltpu.CompilerParams(vmem_limit_bytes=VMEM_LIMIT),
        cost_estimate=pl.CostEstimate(
            flops=4 * (nx + ny) * share * img * half,
            bytes_accessed=4 * img * ((nx + ny) * share + half),
            transcendentals=0,
        ),
        name=f"partial_pieces_{shift}",
    )(place, mine_t, theirs_t, *grads)


def first_sum_kernel(place_ref, *refs):
    for stream in range(2):
        own, one, two, three = refs[4 * stream : 4 * stream + 4]
        for k, out in enumerate(refs[8 + 4 * stream : 12 + 4 * stream]):
            share = out.shape[0]
            rows = pl.ds(pl.multiple_of((place_ref[1 - stream] ^ k) * share, 16), share)
            total = own[rows] + one[rows].astype(F32) + two[rows].astype(F32) + three[rows].astype(F32)
            out[...] = total.astype(out.dtype)


def first_sums(place, firsts, seconds, share):
    half = firsts[0].shape[1]
    outs = ([jax.ShapeDtypeStruct((share, half), F32)] + [jax.ShapeDtypeStruct((share, half), BF16)] * 3) * 2
    return pl.pallas_call(
        first_sum_kernel,
        in_specs=[SMEM] + [VMEM] * 8,
        out_specs=[VMEM] * 8,
        out_shape=outs,
        compiler_params=pltpu.CompilerParams(vmem_limit_bytes=VMEM_LIMIT),
        cost_estimate=pl.CostEstimate(
            flops=32 * share * half, bytes_accessed=100 * share * half, transcendentals=0
        ),
        name="first_sums",
    )(place, *firsts, *seconds)


def second_sum_kernel(place_ref, *refs):
    ones, twos = refs[:4], refs[4:8]
    own_ref, keep_ref, send_ref = refs[8:]
    first = ones[0][...] + sum(r[...].astype(F32) for r in ones[1:])
    second = twos[0][...] + sum(r[...].astype(F32) for r in twos[1:])
    low = place_ref[2] == 0
    own = jnp.where(low, first, second)
    own_ref[...] = own
    keep_ref[...] = own.astype(BF16)
    send_ref[...] = jnp.where(low, second, first).astype(BF16)


def second_sums(place, firsts, seconds):
    share, half = firsts[0].shape
    vmem = pl.BlockSpec(memory_space=pltpu.VMEM)
    return pl.pallas_call(
        second_sum_kernel,
        in_specs=[pl.BlockSpec(memory_space=pltpu.SMEM)] + [vmem] * 8,
        out_specs=[vmem] * 3,
        out_shape=[jax.ShapeDtypeStruct((share, half), kind) for kind in (F32, BF16, BF16)],
        compiler_params=pltpu.CompilerParams(vmem_limit_bytes=VMEM_LIMIT),
        cost_estimate=pl.CostEstimate(
            flops=8 * share * half, bytes_accessed=28 * share * half, transcendentals=0
        ),
        name="second_sums",
    )(place, *firsts, *seconds)


def on_device(shape, llm_grad, route_slot, route_row, pre_act, down_weight):
    nx, ny, nz = shape
    dp = lax.axis_size("dp")
    n_cuts = lax.axis_size("cuts")
    img, hid = pre_act.shape
    half = llm_grad.shape[1] // 2
    cap = 2 * img // dp
    third = cap // 3
    share = 2 * hid // dp
    core_bit, z_bit, y_bit, x_bit = 1, 2, 2 * nz, 2 * nz * ny

    def across(value, mask):
        return lax.ppermute(value, "dp", [(i, i ^ mask) for i in range(dp)])

    def over(value, mask, turn):
        pairs = [
            (c * dp + i, ((c + turn) % n_cuts) * dp + (i ^ mask)) for c in range(n_cuts) for i in range(dp)
        ]
        return lax.ppermute(value, ("cuts", "dp"), pairs)

    me = lax.axis_index("dp").astype(jnp.int32)
    x, y, z, core = me // x_bit, me // y_bit % ny, me // z_bit % nz, me % 2
    place = jnp.stack([x, y, z, core]).astype(jnp.int32)

    their_pre = across(pre_act, core_bit)

    sent = gather_rows(llm_grad, route_slot, route_row, dp, cap)
    sent = sent.reshape(dp, sent.shape[2], 128)
    sent, pre_act, their_pre, down_weight = lax.optimization_barrier((sent, pre_act, their_pre, down_weight))
    got = lax.all_to_all(sent, "dp", 0, 0, tiled=True)

    mine_t, slope = hidden_transposed(pre_act, True)
    (theirs_t,) = hidden_transposed(their_pre, False)
    weight_t = down_weight.T
    got, mine_t, theirs_t, slope, place, weight_t = lax.optimization_barrier(
        (got, mine_t, theirs_t, slope, place, weight_t)
    )
    mine_t = mine_t.reshape(nx, ny, nz, share, img)
    theirs_t = theirs_t.reshape(nx, ny, nz, share, img)

    notes = got[:, half // 128 * 2 * cap :][:, :2, : 2 * cap].astype(jnp.int32)
    landing = notes[:, 0] * 32 + notes[:, 1]
    lane = jnp.arange(4 * third, dtype=jnp.int32)
    landing = jnp.stack(
        [
            jnp.where(lane < cap, landing[:, : 4 * third], -1),
            jnp.where(lane >= third, landing[:, 2 * third :], -1),
        ]
    )
    grads = land_rows(place, got, landing, img, half, cap)

    others = across(grads[1], core_bit)
    firsts, seconds = {}, {}
    for shifts in ((1, 3), (2,), (0,)):
        made = {shift: partial_pieces(mine_t, theirs_t, grads, place, shift) for shift in shifts}
        mine_t, others, made = lax.optimization_barrier((mine_t, others, made))
        for shift, (one, two) in made.items():
            if shift == 2:
                two, seconds[1] = lax.optimization_barrier((two, seconds[1]))
            seconds[shift] = across(two, shift * y_bit) if shift else two
            firsts[shift] = across(one, shift * x_bit) if shift else one

    d_pre = d_pre_product(place, grads[0], others, weight_t, slope)
    firsts[0], seconds[0], d_pre = lax.optimization_barrier((firsts[0], seconds[0], d_pre))

    sums = first_sums(place, [firsts[k] for k in range(4)], [seconds[k] for k in range(4)], share)
    firsts = [sums[0]] + [across(sums[k], k * y_bit) for k in (1, 2, 3)]
    seconds = [sums[4]] + [across(sums[4 + k], k * x_bit) for k in (1, 2, 3)]
    total, keep, send = second_sums(place, firsts, seconds)

    total = total + over(send, z_bit, 0).astype(F32)
    for turn in range(1, n_cuts):
        total = total + over(keep, 0, turn).astype(F32) + over(send, z_bit, turn).astype(F32)

    total = (total * (1.0 / (n_cuts * dp))).reshape(2, share // 2, half)
    mine = jnp.where(core == 0, total[0], total[1])
    other = across(jnp.where(core == 0, total[1], total[0]), core_bit)
    w_grad = jnp.concatenate([jnp.where(core == 0, mine, other), jnp.where(core == 0, other, mine)], axis=1)
    return (d_pre, w_grad)


def solution(mesh):
    placed = (
        P(("cuts", "dp"), None),
        P(("cuts", "dp")),
        P(("cuts", "dp")),
        P(("cuts", "dp"), None),
        P(),
    )
    return jax.shard_map(
        functools.partial(on_device, (4, 4, 2)),
        mesh=mesh,
        in_specs=placed,
        out_specs=(P(("cuts", "dp"), None), P("dp", None)),
        check_vma=False,
    )
```

```python
import functools

import jax
import jax.numpy as jnp
from jax import lax
from jax.experimental import pallas as pl
from jax.experimental.pallas import tpu as pltpu
from jax.sharding import PartitionSpec as P

BF16 = jnp.bfloat16
VMEM = pl.BlockSpec(memory_space=pltpu.VMEM)
SMEM = pl.BlockSpec(memory_space=pltpu.SMEM)
F32 = jnp.float32
VMEM_LIMIT = 28 * 1024 * 1024
VMEM_LARGE = 54 * 1024 * 1024
VMEM_DPRE = 50 * 1024 * 1024
LANES = 512


def gelu_parts(pre_value):
    normal_cdf = 0.5 * (1.0 + lax.erf(pre_value * 0.7071067811865476))
    normal_pdf = jnp.exp(-0.5 * pre_value * pre_value) * 0.3989422804014327
    return (pre_value * normal_cdf, normal_cdf + pre_value * normal_pdf)


def dot32(a, b, contract=((1,), (0,))):
    return lax.dot_general(a, b, (contract, ((), ())), preferred_element_type=F32)


def slot_order(place, third):
    return jnp.where(
        place < 3 * third, place, jnp.where(place < 4 * third, place + 2 * third, place - third)
    )


def gather_kernel(third, slot_ref, row_ref, grad_ref, sent_ref, pick_ref, tile_ref, note_ref, tile_sem, note_sem):
    part = pl.program_id(0)
    last = pl.num_programs(0) - 1
    bank = lax.rem(part, 2)
    block = 6 * third
    steps, rows_per = pick_ref.shape[:2]
    chips = rows_per // block
    tiles = sent_ref.shape[2] // block

    def tile_copy(number, side):
        tile = 2 * number + side
        core = lax.div(tile, tiles)
        rows = pl.ds(pl.multiple_of(lax.rem(tile, tiles) * block, 16), block)
        return pltpu.make_async_copy(
            tile_ref.at[lax.rem(number, 2), side], sent_ref.at[:, core, rows, :], tile_sem.at[lax.rem(number, 2), side]
        )

    def note_copy(core):
        return pltpu.make_async_copy(
            note_ref, sent_ref.at[:, core, pl.ds(tiles * block, 16), :], note_sem.at[core]
        )

    @pl.when(part >= 2)
    def _():
        for side in range(2):
            tile_copy(part - 2, side).wait()

    def emit(step, pick):
        rows = dot32(pick, grad_ref[...]).astype(BF16)
        for side in range(2):
            half = rows[:, side * 128 : side * 128 + 128]
            tile_ref[bank, side, pl.ds(step * chips, chips)] = half.reshape(chips, block, 128)

    @pl.when(part == 0)
    def _():
        note_ref[...] = jnp.zeros_like(note_ref)
        line = lax.broadcasted_iota(jnp.int32, (16, block), 0)
        slots, numbers = (
            jnp.concatenate([ref[at : at + 1, :] for at in range(ref.shape[0])], axis=1)
            for ref in (slot_ref, row_ref)
        )
        for step in range(steps):
            row = lax.broadcasted_iota(jnp.int32, (rows_per, 1), 0) + step * rows_per
            place = lax.rem(row, block)
            slot = row - place + slot_order(place, third)
            match = slot == slots
            pick = jnp.where(match, 1.0, 0.0).astype(BF16)
            pick_ref[step] = pick
            emit(step, pick)
            number = jnp.sum(jnp.where(match, numbers + 1, 0).astype(F32), axis=1, keepdims=True)
            for chip in range(chips):
                wide = jnp.broadcast_to(number[chip * block : (chip + 1) * block], (block, 128))
                flat = wide.T[:16].astype(jnp.int32) - 1
                note = jnp.where(line == 0, flat >> 5, flat & 31).astype(F32).astype(BF16)
                note_ref[step * chips + chip, :, :block] = note
        for core in range(2):
            note_copy(core).start()

    @pl.when(part > 0)
    def _():
        for step in range(steps):
            emit(step, pick_ref[step])

    for side in range(2):
        tile_copy(part, side).start()

    @pl.when(part == last)
    def _():
        for side in range(2):
            tile_copy(part - 1, side).wait()
            tile_copy(part, side).wait()
            note_copy(side).wait()


def gather_rows(llm_grad, route_slot, route_row, dp, cap):
    rows, feat = llm_grad.shape
    half = feat // 2
    slots = dp * cap
    chips = dp // 2
    steps = 8
    return pl.pallas_call(
        functools.partial(gather_kernel, cap // 3),
        grid=(feat // 256,),
        in_specs=[
            pl.BlockSpec((rows // 128, 128), lambda n: (0, 0)),
            pl.BlockSpec((rows // 128, 128), lambda n: (0, 0)),
            pl.BlockSpec((rows, 256), lambda n: (0, n)),
        ],
        out_specs=pl.BlockSpec(memory_space=pltpu.HBM),
        out_shape=pltpu.HBM((chips, 2, half // 128 * 2 * cap + 16, 128), BF16),
        scratch_shapes=[
            pltpu.VMEM((steps, slots // steps, rows), BF16),
            pltpu.VMEM((2, 2, chips, 2 * cap, 128), BF16),
            pltpu.VMEM((chips, 16, 128), BF16),
            pltpu.SemaphoreType.DMA((2, 2)),
            pltpu.SemaphoreType.DMA((2,)),
        ],
        compiler_params=pltpu.CompilerParams(vmem_limit_bytes=VMEM_LARGE),
        cost_estimate=pl.CostEstimate(
            flops=2 * slots * rows * feat, bytes_accessed=2 * (rows + slots) * feat, transcendentals=0
        ),
        name="gather_rows",
    )(route_slot.reshape(rows // 128, 128), route_row.reshape(rows // 128, 128), llm_grad)


def land_kernel(place_ref, got_ref, land_ref, mine_ref, theirs_ref, pick_ref):
    part = pl.program_id(0)
    last = pl.num_programs(0) - 1
    senders, block, _ = got_ref.shape
    block = block // 2
    span = 2 * block // 3
    img = mine_ref.shape[0]
    outs = (mine_ref, theirs_ref)

    def rows(side, tile):
        begin = pl.multiple_of((side ^ place_ref[3]) * (block - span) + tile * block, 16)
        return got_ref[:, pl.ds(begin, span), :].reshape(senders * span, 128)

    def both(side):
        return jnp.concatenate([rows(side, 0), rows(side, 1)], axis=1)

    @pl.when(part == 0)
    def _():
        count = img // 4
        for side in range(2):
            right = both(side)
            land = land_ref[side ^ place_ref[3]]
            for begin in range(0, img, count):
                row = lax.broadcasted_iota(jnp.int32, (count, 1), 0) + begin
                pick = jnp.where(row == land, 1.0, 0.0).astype(BF16)
                pick_ref[side, begin : begin + count] = pick
                outs[side][begin : begin + count] = dot32(pick, right).astype(BF16)

    @pl.when((part > 0) & (part < last))
    def _():
        for side in range(2):
            outs[side][...] = dot32(pick_ref[side], both(side)).astype(BF16)

    @pl.when(part == last)
    def _():
        for side in range(2):
            outs[side][:, :128] = dot32(pick_ref[side], rows(side, 0)).astype(BF16)


def land_rows(place, got, landing, img, half, cap):
    dp = got.shape[0]
    span = 4 * cap // 3
    return pl.pallas_call(
        land_kernel,
        grid_spec=pltpu.PrefetchScalarGridSpec(
            num_scalar_prefetch=1,
            grid=(pl.cdiv(half, 256),),
            in_specs=[
                pl.BlockSpec((dp, 4 * cap, 128), lambda n, p: (0, n, 0)),
                pl.BlockSpec((2, 1, dp * span), lambda n, p: (0, 0, 0)),
            ],
            out_specs=[pl.BlockSpec((img, 256), lambda n, p: (0, n))] * 2,
            scratch_shapes=[pltpu.VMEM((2, img, dp * span), BF16)],
        ),
        out_shape=[jax.ShapeDtypeStruct((img, half), BF16)] * 2,
        compiler_params=pltpu.CompilerParams(vmem_limit_bytes=VMEM_LIMIT),
        cost_estimate=pl.CostEstimate(
            flops=4 * img * dp * span * half, bytes_accessed=4 * half * (dp * cap + img), transcendentals=0
        ),
        name="land_rows",
    )(place, got, landing.reshape(2, 1, dp * span))


def hidden_kernel(pre_ref, out_ref, *slope_ref):
    value, slope = gelu_parts(pre_ref[...].astype(F32))
    out_ref[...] = value.T.astype(BF16)
    if slope_ref:
        slope_ref[0][...] = slope


def hidden_transposed(pre_act, with_slope):
    img, hid = pre_act.shape
    out = [(pl.BlockSpec((256, img), lambda n: (n, 0)), jax.ShapeDtypeStruct((hid, img), BF16))]
    if with_slope:
        out.append((pl.BlockSpec((img, 256), lambda n: (0, n)), pltpu.HBM((img, hid), F32)))
    return pl.pallas_call(
        hidden_kernel,
        grid=(hid // 256,),
        in_specs=[pl.BlockSpec((img, 256), lambda n: (0, n))],
        out_specs=[spec for spec, _ in out],
        out_shape=[kind for _, kind in out],
        compiler_params=pltpu.CompilerParams(vmem_limit_bytes=VMEM_LARGE),
        cost_estimate=pl.CostEstimate(
            flops=30 * img * hid, bytes_accessed=4 * img * hid, transcendentals=img * hid
        ),
        name="hidden_transposed",
    )(pre_act)


def d_pre_kernel(place_ref, mine_ref, theirs_ref, weight_ref, slope_ref, out_ref, both_ref):
    half = mine_ref.shape[1]

    @pl.when(pl.program_id(0) == 0)
    def _():
        core = place_ref[3]
        both_ref[:, pl.ds(pl.multiple_of(core * half, 128), half)] = mine_ref[...]
        both_ref[:, pl.ds(pl.multiple_of((1 - core) * half, 128), half)] = theirs_ref[...]

    for at in range(0, LANES, 256):
        lane = slice(at, at + 256)
        total = dot32(both_ref[...], weight_ref[:, lane])
        out_ref[:, lane] = (total * slope_ref[:, lane]).astype(BF16)


def d_pre_product(place, mine, theirs, weight_t, slope):
    img, half = mine.shape
    hid = weight_t.shape[1]
    return pl.pallas_call(
        d_pre_kernel,
        grid_spec=pltpu.PrefetchScalarGridSpec(
            num_scalar_prefetch=1,
            grid=(hid // LANES,),
            in_specs=[
                VMEM,
                VMEM,
                pl.BlockSpec((2 * half, LANES), lambda n, p: (0, n)),
                pl.BlockSpec((img, LANES), lambda n, p: (0, n)),
            ],
            out_specs=pl.BlockSpec((img, LANES), lambda n, p: (0, n)),
            scratch_shapes=[pltpu.VMEM((img, 2 * half), BF16)],
        ),
        out_shape=pltpu.HBM((img, hid), BF16),
        compiler_params=pltpu.CompilerParams(vmem_limit_bytes=VMEM_DPRE),
        cost_estimate=pl.CostEstimate(
            flops=4 * img * half * hid, bytes_accessed=4 * hid * half + 6 * img * hid, transcendentals=0
        ),
        name="d_pre",
    )(place, mine, theirs, weight_t, slope)


def partial_kernel(shift, place_ref, mine_ref, theirs_ref, near_ref, far_ref, first_ref, second_ref):
    img = near_ref.shape[0]
    for stream, out in enumerate((first_ref, second_ref)):
        at = place_ref[stream] ^ shift
        total = 0.0
        for left, grad in ((mine_ref, near_ref), (theirs_ref, far_ref)):
            block = left[:, at, 1] if stream else left[at, :, 0]
            total = total + dot32(block.reshape(out.shape[0], img), grad[...])
        out[...] = total.astype(out.dtype)


def partial_pieces(mine_t, theirs_t, grads, place, shift):
    nx, ny, _, share, img = mine_t.shape
    half = grads[0].shape[1]
    return pl.pallas_call(
        functools.partial(partial_kernel, shift),
        in_specs=[SMEM] + [VMEM] * 4,
        out_specs=[VMEM] * 2,
        out_shape=[jax.ShapeDtypeStruct((n * share, half), BF16 if shift else F32) for n in (ny, nx)],
        compiler_params=pltpu.CompilerParams(vmem_limit_bytes=VMEM_LIMIT),
        cost_estimate=pl.CostEstimate(
            flops=4 * (nx + ny) * share * img * half,
            bytes_accessed=4 * img * ((nx + ny) * share + half),
            transcendentals=0,
        ),
        name=f"partial_pieces_{shift}",
    )(place, mine_t, theirs_t, *grads)


def first_sum_kernel(place_ref, *refs):
    for stream in range(2):
        own, one, two, three = refs[4 * stream : 4 * stream + 4]
        for k, out in enumerate(refs[8 + 4 * stream : 12 + 4 * stream]):
            share = out.shape[0]
            rows = pl.ds(pl.multiple_of((place_ref[1 - stream] ^ k) * share, 16), share)
            total = own[rows] + one[rows].astype(F32) + two[rows].astype(F32) + three[rows].astype(F32)
            out[...] = total.astype(out.dtype)


def first_sums(place, firsts, seconds, share):
    half = firsts[0].shape[1]
    outs = ([jax.ShapeDtypeStruct((share, half), F32)] + [jax.ShapeDtypeStruct((share, half), BF16)] * 3) * 2
    return pl.pallas_call(
        first_sum_kernel,
        in_specs=[SMEM] + [VMEM] * 8,
        out_specs=[VMEM] * 8,
        out_shape=outs,
        compiler_params=pltpu.CompilerParams(vmem_limit_bytes=VMEM_LIMIT),
        cost_estimate=pl.CostEstimate(
            flops=32 * share * half, bytes_accessed=100 * share * half, transcendentals=0
        ),
        name="first_sums",
    )(place, *firsts, *seconds)


def second_sum_kernel(place_ref, *refs):
    ones, twos = refs[:4], refs[4:8]
    own_ref, keep_ref, send_ref = refs[8:]
    first = ones[0][...] + sum(r[...].astype(F32) for r in ones[1:])
    second = twos[0][...] + sum(r[...].astype(F32) for r in twos[1:])
    low = place_ref[2] == 0
    own = jnp.where(low, first, second)
    own_ref[...] = own
    keep_ref[...] = own.astype(BF16)
    send_ref[...] = jnp.where(low, second, first).astype(BF16)


def second_sums(place, firsts, seconds):
    share, half = firsts[0].shape
    vmem = pl.BlockSpec(memory_space=pltpu.VMEM)
    return pl.pallas_call(
        second_sum_kernel,
        in_specs=[pl.BlockSpec(memory_space=pltpu.SMEM)] + [vmem] * 8,
        out_specs=[vmem] * 3,
        out_shape=[jax.ShapeDtypeStruct((share, half), kind) for kind in (F32, BF16, BF16)],
        compiler_params=pltpu.CompilerParams(vmem_limit_bytes=VMEM_LIMIT),
        cost_estimate=pl.CostEstimate(
            flops=8 * share * half, bytes_accessed=28 * share * half, transcendentals=0
        ),
        name="second_sums",
    )(place, *firsts, *seconds)


def on_device(shape, llm_grad, route_slot, route_row, pre_act, down_weight):
    nx, ny, nz = shape
    dp = lax.axis_size("dp")
    n_cuts = lax.axis_size("cuts")
    img, hid = pre_act.shape
    half = llm_grad.shape[1] // 2
    cap = 2 * img // dp
    third = cap // 3
    share = 2 * hid // dp
    core_bit, z_bit, y_bit, x_bit = 1, 2, 2 * nz, 2 * nz * ny

    def across(value, mask):
        return lax.ppermute(value, "dp", [(i, i ^ mask) for i in range(dp)])

    def over(value, mask, turn):
        pairs = [
            (c * dp + i, ((c + turn) % n_cuts) * dp + (i ^ mask)) for c in range(n_cuts) for i in range(dp)
        ]
        return lax.ppermute(value, ("cuts", "dp"), pairs)

    me = lax.axis_index("dp").astype(jnp.int32)
    x, y, z, core = me // x_bit, me // y_bit % ny, me // z_bit % nz, me % 2
    place = jnp.stack([x, y, z, core]).astype(jnp.int32)

    their_pre = across(pre_act, core_bit)

    sent = gather_rows(llm_grad, route_slot, route_row, dp, cap)
    sent = sent.reshape(dp, sent.shape[2], 128)
    sent, pre_act, their_pre, down_weight = lax.optimization_barrier((sent, pre_act, their_pre, down_weight))
    got = lax.all_to_all(sent, "dp", 0, 0, tiled=True)

    mine_t, slope = hidden_transposed(pre_act, True)
    (theirs_t,) = hidden_transposed(their_pre, False)
    weight_t = down_weight.T
    got, mine_t, theirs_t, slope, place, weight_t = lax.optimization_barrier(
        (got, mine_t, theirs_t, slope, place, weight_t)
    )
    mine_t = mine_t.reshape(nx, ny, nz, share, img)
    theirs_t = theirs_t.reshape(nx, ny, nz, share, img)

    notes = got[:, half // 128 * 2 * cap :][:, :2, : 2 * cap].astype(jnp.int32)
    landing = notes[:, 0] * 32 + notes[:, 1]
    landing = jnp.where(landing >= 0, landing, -1)
    lane = jnp.arange(4 * third, dtype=jnp.int32)
    landing = jnp.stack(
        [
            jnp.where(lane < cap, landing[:, : 4 * third], -1),
            jnp.where(lane >= third, landing[:, 2 * third :], -1),
        ]
    )
    grads = land_rows(place, got, landing, img, half, cap)

    others = across(grads[1], core_bit)
    firsts, seconds = {}, {}
    for shifts in ((1, 3), (2,), (0,)):
        made = {shift: partial_pieces(mine_t, theirs_t, grads, place, shift) for shift in shifts}
        mine_t, others, made = lax.optimization_barrier((mine_t, others, made))
        for shift, (one, two) in made.items():
            firsts[shift] = across(one, shift * x_bit) if shift else one
            seconds[shift] = across(two, shift * y_bit) if shift else two

    d_pre = d_pre_product(place, grads[0], others, weight_t, slope)
    firsts[0], seconds[0], d_pre = lax.optimization_barrier((firsts[0], seconds[0], d_pre))

    sums = first_sums(place, [firsts[k] for k in range(4)], [seconds[k] for k in range(4)], share)
    firsts, seconds = [sums[0]], [sums[4]]
    for k in (1, 3, 2):
        firsts.append(across(sums[k], k * y_bit))
        seconds.append(across(sums[4 + k], k * x_bit))
    total, keep, send = second_sums(place, firsts, seconds)

    total = total + over(send, z_bit, 0).astype(F32)
    for turn in range(1, n_cuts):
        total = total + over(keep, 0, turn).astype(F32) + over(send, z_bit, turn).astype(F32)

    total = (total * (1.0 / (n_cuts * dp))).reshape(2, share // 2, half)
    mine = jnp.where(core == 0, total[0], total[1])
    other = across(jnp.where(core == 0, total[1], total[0]), core_bit)
    w_grad = jnp.concatenate([jnp.where(core == 0, mine, other), jnp.where(core == 0, other, mine)], axis=1)
    return (d_pre, w_grad)


def solution(mesh):
    placed = (
        P(("cuts", "dp"), None),
        P(("cuts", "dp")),
        P(("cuts", "dp")),
        P(("cuts", "dp"), None),
        P(),
    )
    return jax.shard_map(
        functools.partial(on_device, (4, 4, 2)),
        mesh=mesh,
        in_specs=placed,
        out_specs=(P(("cuts", "dp"), None), P("dp", None)),
        check_vma=False,
    )
```
